256 devices in a mesh: wide: 32 (over z, y), narrow: 8 (over x, core).
Axes of the slice: x: 4, y: 4, z: 8, core: 2. Of those that a mesh axis runs over, the one named last changes fastest.
Arguments:
- thermal_correction: float32 [1024, 32, 1024], P(('wide', 'narrow')), may hold values from -6 to 6
- forcing_vector: float32 [1024, 32, 1024], P(('wide', 'narrow')), may hold values from -6 to 6
- thermal_transfer_factor: float32 [1024, 32, 1024], P(('wide', 'narrow')), may hold values from 0.3 to 30
- heat_storage_factor: float32 [1024, 32, 1024], P(('wide', 'narrow')), may hold values from 0.1 to 1
- wall_status_code: int32 [1024, 32, 1024], P(('wide', 'narrow')), may hold values from 0 to 2
- block_holder_chip: int32 [768], replicated, may hold values from 0 to 255, as said below
Outputs:
- relaxed_heat_level: float32 [1024, 32, 1024], P(('wide', 'narrow'))
- defect_restricted_grid: float32 [256, 32, 1024], P(('wide', 'narrow'))
The draws below stay inside these ranges and needn't reach their ends.
Inputs may be any that keep to these rules, and one draw needn't show every extreme that they name: block_holder_chip never falls along the patches; every device owns a run of 2 to 4 consecutive patches, one device exactly 4; the devices' counts come in pairs that sum to 6.
All inputs are finite; a program needn't handle non-finite values.
Results may differ from the reference program's by a relative error of at most 0.0003.
Values sent between devices are 32-bit elements; how exact they have to be, the bound alone decides.
No kernel may reach another device: no remote copies, remote signals or barrier semaphores. Data moves between devices by JAX's collectives and lax.ppermute only.
A program may use at most 192 MiB of HBM per device.

```python
import math
import jax
import jax.numpy as jnp
from jax import lax

BLOCK_SPAN_SITES = 32
PATCH_DEV = 3
SWEEPS = 2
CHIP_BOX_COUNT = 4
CSLOTS = 1
NPATCH = 768
NCOARSE = 96
DEVICES = 256


def device_counts(key):
    base = jax.random.fold_in(key, 501)
    ordering = jax.random.permutation(jax.random.fold_in(base, 1), DEVICES).astype(jnp.int32)
    surplus = jax.random.randint(jax.random.fold_in(base, 2), (DEVICES // 2,), 0, PATCH_DEV - 1)
    surplus = surplus.at[0].set(PATCH_DEV - 2)
    paired = jnp.stack([PATCH_DEV + surplus, PATCH_DEV - surplus], axis=1).reshape(DEVICES)
    return jnp.zeros((DEVICES,), jnp.int32).at[ordering].set(paired.astype(jnp.int32))


def draw_block_holder_chip(key, part):
    counts = device_counts(key)
    ending = jnp.cumsum(counts)
    ordinal = jnp.arange(NPATCH, dtype=jnp.int32)
    return jnp.sum((ending[None, :] <= ordinal[:, None]).astype(jnp.int32), axis=1).astype(jnp.int32)


def draw_wall_status_code(key, part):
    counts = device_counts(key)
    key = jax.random.fold_in(key, 23)
    total_rows = DEVICES * CHIP_BOX_COUNT
    row_index = jnp.arange(total_rows, dtype=jnp.int32)
    owner = row_index // CHIP_BOX_COUNT
    within = row_index % CHIP_BOX_COUNT
    held = counts[owner]
    cut_count = (held + 2) // 3
    is_cut = within < cut_count
    lead = jax.random.randint(jax.random.fold_in(key, 1), (total_rows,), 1, 3)
    facing = 2 * jax.random.randint(jax.random.fold_in(key, 2), (total_rows,), 0, 2) - 1
    second = jax.random.randint(jax.random.fold_in(key, 3), (total_rows,), -2, 3)
    third = jax.random.randint(jax.random.fold_in(key, 4), (total_rows,), -2, 3)
    anchor = jax.random.randint(jax.random.fold_in(key, 5), (total_rows,), BLOCK_SPAN_SITES // 4, 3 * BLOCK_SPAN_SITES // 4 + 1)
    thick = lead + jnp.abs(second) + jnp.abs(third)
    xpos = jnp.arange(BLOCK_SPAN_SITES, dtype=jnp.int32)[None, :, None]
    cols = jnp.arange(BLOCK_SPAN_SITES * BLOCK_SPAN_SITES, dtype=jnp.int32)[None, None, :]
    ypos = cols // BLOCK_SPAN_SITES
    zpos = cols % BLOCK_SPAN_SITES
    level = facing[:, None, None] * lead[:, None, None] * (xpos - anchor[:, None, None]) + second[:, None, None] * (ypos - BLOCK_SPAN_SITES // 2) + third[:, None, None] * (zpos - BLOCK_SPAN_SITES // 2)
    kind = jnp.where(level < 0, 2, jnp.where(level < thick[:, None, None], 1, 0))
    return jnp.where(is_cut[:, None, None], kind, 0).astype(jnp.int32)


def level_of(key, extent, split, low, top_value):
    loudness, own = 1.0, jax.random.fold_in(key, 6)
    for axis_at, blocks in split:
        heights = jnp.exp(jax.random.uniform(jax.random.fold_in(own, axis_at), (blocks,), jnp.float32, low / len(split), top_value / len(split)))
        loudness = loudness * jnp.repeat(heights, extent[axis_at] // blocks).reshape([-1 if axis == axis_at else 1 for axis in range(len(extent))])
    return loudness


def noise(own_key, shape, scale, limit, cuts=(), held_as=jnp.bfloat16):
    drawn = jax.random.normal(own_key, shape, jnp.float32) * scale
    if len(cuts) > 0:
        drawn = level_of(own_key, shape, cuts, -0.22, 0.18) * drawn
    return jnp.clip(drawn, min=-limit, max=limit).astype(held_as)


def setup_inputs(seed: int = 0) -> dict:
    arg_keys = jax.random.split(jax.random.key(seed), 7)
    return {
        "thermal_correction": noise(arg_keys[0], (DEVICES * CHIP_BOX_COUNT, BLOCK_SPAN_SITES, BLOCK_SPAN_SITES * BLOCK_SPAN_SITES), 1.0, 6.0, ((0, 256),), jnp.float32),
        "forcing_vector": noise(arg_keys[1], (DEVICES * CHIP_BOX_COUNT, BLOCK_SPAN_SITES, BLOCK_SPAN_SITES * BLOCK_SPAN_SITES), 1.0, 6.0, ((0, 256),), jnp.float32),
        "thermal_transfer_factor": jnp.clip(jnp.exp(math.log(30.0) - 4.6051701 * jax.random.uniform(arg_keys[2], (DEVICES * CHIP_BOX_COUNT, BLOCK_SPAN_SITES, BLOCK_SPAN_SITES * BLOCK_SPAN_SITES), jnp.float32) ** level_of(arg_keys[2], (DEVICES * CHIP_BOX_COUNT, BLOCK_SPAN_SITES, BLOCK_SPAN_SITES * BLOCK_SPAN_SITES), ((0, 256),), -0.2, 0.2)), 0.3, 30.0),
        "heat_storage_factor": jnp.clip(jnp.exp(math.log(1.0) - 2.3025851 * jax.random.uniform(arg_keys[3], (DEVICES * CHIP_BOX_COUNT, BLOCK_SPAN_SITES, BLOCK_SPAN_SITES * BLOCK_SPAN_SITES), jnp.float32) ** level_of(arg_keys[3], (DEVICES * CHIP_BOX_COUNT, BLOCK_SPAN_SITES, BLOCK_SPAN_SITES * BLOCK_SPAN_SITES), ((0, 256),), -0.2, 0.2)), 0.1, 1.0),
        "wall_status_code": draw_wall_status_code(jax.random.fold_in(arg_keys[6], 71), 0),
        "block_holder_chip": draw_block_holder_chip(jax.random.fold_in(arg_keys[6], 71), 0),
    }


def storage_rows(holders, stride):
    entries = holders.shape[0]
    ordinal = jnp.arange(entries, dtype=jnp.int32)
    opening = jnp.concatenate([jnp.ones((1,), dtype=bool), holders[1:] != holders[:-1]])
    leading = lax.cummax(jnp.where(opening, ordinal, 0), axis=0)
    return (holders * stride + ordinal - leading).astype(jnp.int32)


def output_mesh_view(values, matrix_line_terms):
    picked = values[matrix_line_terms]
    picked = picked.reshape(NPATCH // 4, 2, 2, BLOCK_SPAN_SITES, BLOCK_SPAN_SITES, BLOCK_SPAN_SITES)
    picked = picked.transpose(2, 3, 1, 4, 0, 5)
    return picked.reshape(2 * BLOCK_SPAN_SITES, 2 * BLOCK_SPAN_SITES, (NPATCH // 4) * BLOCK_SPAN_SITES)


def input_mesh_view(grid, matrix_line_terms, count):
    pieces = grid.reshape(2, BLOCK_SPAN_SITES, 2, BLOCK_SPAN_SITES, NPATCH // 4, BLOCK_SPAN_SITES)
    pieces = pieces.transpose(4, 2, 0, 1, 3, 5).reshape(NPATCH, BLOCK_SPAN_SITES, BLOCK_SPAN_SITES * BLOCK_SPAN_SITES)
    return jnp.zeros((count, BLOCK_SPAN_SITES, BLOCK_SPAN_SITES * BLOCK_SPAN_SITES), jnp.float32).at[matrix_line_terms].set(pieces)


def shifted(values, dimension, offset, padding):
    widths = [(0, 0), (0, 0), (0, 0)]
    widths[dimension] = (1, 1)
    if padding is None:
        padded = jnp.pad(values, widths, mode="edge")
    else:
        padded = jnp.pad(values, widths, constant_values=padding)
    length = values.shape[dimension]
    return lax.slice_in_dim(padded, 1 + offset, 1 + offset + length, axis=dimension)


def gathered(values, coefficients):
    summed = None
    number = 0
    for dimension in range(3):
        for offset in (-1, 1):
            term = coefficients[number] * shifted(values, dimension, offset, 0.0)
            summed = term if summed is None else summed + term
            number = number + 1
    return summed


def reference(thermal_correction, forcing_vector, thermal_transfer_factor, heat_storage_factor, wall_status_code, block_holder_chip):
    matrix_line_terms = storage_rows(block_holder_chip, CHIP_BOX_COUNT)
    current_estimate = output_mesh_view(thermal_correction, matrix_line_terms)
    forcing = output_mesh_view(forcing_vector, matrix_line_terms)
    heat = output_mesh_view(thermal_transfer_factor, matrix_line_terms)
    storage = output_mesh_view(heat_storage_factor, matrix_line_terms)
    kinds = output_mesh_view(wall_status_code, matrix_line_terms)
    aperture = jnp.where(kinds == 0, 1.0, jnp.where(kinds == 1, 0.5, 0.0)).astype(jnp.float32)
    coefficients = []
    for dimension in range(3):
        for offset in (-1, 1):
            remote_heat = shifted(heat, dimension, offset, None)
            remote_open = shifted(aperture, dimension, offset, 1.0)
            coefficients.append(aperture * remote_open * (2.0 * heat * remote_heat) / (heat + remote_heat))
    summed = coefficients[0]
    for number in range(1, 6):
        summed = summed + coefficients[number]
    diagonal = jnp.where(kinds == 2, 1.0, storage + summed + jnp.where(kinds == 1, heat, 0.0))
    array_extent = current_estimate.shape
    colour = (lax.broadcasted_iota(jnp.int32, array_extent, 0) + lax.broadcasted_iota(jnp.int32, array_extent, 1)
              + lax.broadcasted_iota(jnp.int32, array_extent, 2)) % 2
    for sweep_index in range(SWEEPS):
        for shade in (0, 1):
            updated = (forcing + gathered(current_estimate, coefficients)) / diagonal
            current_estimate = jnp.where(colour == shade, updated, current_estimate)
    residual = forcing - (diagonal * current_estimate - gathered(current_estimate, coefficients))
    relaxed_heat_level = input_mesh_view(current_estimate, matrix_line_terms, DEVICES * CHIP_BOX_COUNT)
    coarse = residual.reshape(BLOCK_SPAN_SITES, 2, BLOCK_SPAN_SITES, 2, NCOARSE * BLOCK_SPAN_SITES, 2).mean(axis=(1, 3, 5))
    coarse = coarse.reshape(BLOCK_SPAN_SITES, BLOCK_SPAN_SITES, NCOARSE, BLOCK_SPAN_SITES).transpose(2, 0, 1, 3)
    coarse = coarse.reshape(NCOARSE, BLOCK_SPAN_SITES, BLOCK_SPAN_SITES * BLOCK_SPAN_SITES)
    coarse_rows = storage_rows(block_holder_chip[0::8], CSLOTS)
    defect_restricted_grid = jnp.zeros((DEVICES * CSLOTS, BLOCK_SPAN_SITES, BLOCK_SPAN_SITES * BLOCK_SPAN_SITES), jnp.float32).at[coarse_rows].set(coarse)
    return relaxed_heat_level, defect_restricted_grid
```

```python
import functools

import jax
import jax.numpy as jnp
from jax import lax
from jax.experimental import pallas as pl
from jax.experimental.pallas import tpu as pltpu
from jax.sharding import PartitionSpec as P

AXES = ("wide", "narrow")
SPAN = 32
LAYER = 1024
SLOTS = 4
TILES = 4
COLS = 8
F32 = jnp.float32
VMEM = pl.BlockSpec(memory_space=pltpu.VMEM)
SMEM = pl.BlockSpec(memory_space=pltpu.SMEM)
FACES = jax.ShapeDtypeStruct((4, SPAN, 128), F32)
FIELD = jax.ShapeDtypeStruct((SLOTS, SPAN, LAYER), F32)


def lanes():
    return lax.broadcasted_iota(jnp.int32, (8, 128), 1)


def sublanes():
    return lax.broadcasted_iota(jnp.int32, (8, 128), 0)


def pick(tile, index):
    return jnp.take_along_axis(tile, index, axis=1, mode="promise_in_bounds")


def turned(tile, by):
    return pltpu.roll(tile, by, axis=1)


def tile_at(ref, xt, j):
    return ref[pl.ds(8 * xt, 8), pl.ds(128 * j, 128)]


def whereabouts(scalars):
    core = scalars[4]
    first, last = scalars[0], scalars[2]
    extra = last - first - 4
    base = jnp.where(core == 0, first, last - 4)
    return core, base, extra


def place(base, s):
    p = base + s
    return lax.rem(p, 2), lax.rem(lax.div(p, 2), 2), lax.div(p, 4)


def extract(s, xt, tiles, iy, faces):
    lane = lanes()
    here = lane // 32 == s
    rows = pl.ds(8 * xt, 8)
    for face, column in ((0, 0), (1, 31)):
        index = 32 * (lane % 4) + column
        found = pick(tiles[0], index)
        for j in range(1, COLS):
            found = jnp.where((lane % 32) // 4 == j, pick(tiles[j], index), found)
        faces[face, rows, :] = jnp.where(here, found, faces[face, rows, :])
    side = jnp.where(iy == 1, tiles[0], tiles[COLS - 1])
    side = turned(side, lax.rem(32 * s + 32 * (1 - iy), 128))
    faces[2, rows, :] = jnp.where(here, side, faces[2, rows, :])


def extract_row(s, j, first, last, ix, faces):
    faces[3, pl.ds(8 * s + j, 1), :] = jnp.where(ix == 1, first[0:1, :], last[7:8, :])


def ghosts(where, own, oth, far, post, out):
    core, base, extra = where
    lane = lanes()
    low = core == 0
    start = jnp.where(low, 4 - extra, extra)
    back = lax.rem(128 - 32 * start, 128)
    cut = 128 - 32 * start

    def window(face, rows):
        a, b = oth[face, rows, :], post[face, rows, :]
        lead = turned(jnp.where(low, a, b), back)
        tail = turned(jnp.where(low, b, a), back)
        return jnp.where(lane < cut, lead, tail)

    iy = ((base + lane // 32) // 2) % 2
    for xt in range(TILES):
        rows = pl.ds(8 * xt, 8)
        mid = window(core, rows)
        edge = far[1 - core, rows, :]
        out[0, rows, :] = jnp.where(low, edge, mid)
        out[1, rows, :] = jnp.where(low, mid, edge)
        mid = window(2, rows)
        edge = far[2, rows, :]
        below = turned(jnp.where(low, edge, mid), 64)
        above = turned(jnp.where(low, mid, edge), 64)
        inner = turned(own[2, rows, :], 64)
        out[2, rows, :] = jnp.where(
            iy == 1, jnp.where(lane < 64, below, inner), jnp.where(lane < 64, inner, above)
        )
    slot = jnp.where(low, start, start + 3)
    from_lead = slot < 4
    row = pl.ds(pl.multiple_of(8 * lax.rem(slot, 4), 8), 8)
    mid = jnp.where(low == from_lead, oth[3, row, :], post[3, row, :])
    below = jnp.where(low, far[3, 24:32, :], mid)
    above = jnp.where(low, mid, far[3, 0:8, :])
    for s in range(SLOTS):
        ix = lax.rem(base + s, 2)
        before = below if s == 0 else own[3, 8 * s - 8 : 8 * s, :]
        after = above if s == SLOTS - 1 else own[3, 8 * s + 8 : 8 * s + 16, :]
        out[3, 8 * s : 8 * s + 8, :] = jnp.where(ix == 1, before, after)


def pad(s, ref, ghost, padded):
    for xt in range(TILES):
        padded[8 + 8 * xt : 16 + 8 * xt, :] = ref[s, pl.ds(8 * xt, 8), :]
    for j in range(COLS):
        row = ghost[3, pl.ds(8 * s + j, 1), :]
        padded[7:8, 128 * j : 128 * j + 128] = row
        padded[40:41, 128 * j : 128 * j + 128] = row


def around(s, xt, padded, ghost):
    lane = lanes()
    rows = pl.ds(8 * xt, 8)
    own = [padded[8 + 8 * xt : 16 + 8 * xt, 128 * j : 128 * j + 128] for j in range(COLS)]
    up = [turned(t, 32) for t in own]
    down = [turned(t, 96) for t in own]
    side = ghost[2, rows, :]
    up_edge = turned(side, lax.rem(128 - 32 * s, 128))
    down_edge = turned(side, lax.rem(224 - 32 * s, 128))
    z_low = turned(ghost[0, rows, :], lax.rem(128 - 32 * s, 128))
    z_high = turned(ghost[1, rows, :], lax.rem(128 - 32 * s, 128))
    result = []
    for j in range(COLS):
        cols = slice(128 * j, 128 * j + 128)
        spread = 4 * j + lane // 32
        result.append(
            (
                padded[7 + 8 * xt : 15 + 8 * xt, cols],
                padded[9 + 8 * xt : 17 + 8 * xt, cols],
                jnp.where(lane < 32, up[j - 1] if j else up_edge, up[j]),
                jnp.where(lane >= 96, down[j + 1] if j < COLS - 1 else down_edge, down[j]),
                jnp.where(lane % 32 == 0, pick(z_low, spread), turned(own[j], 1)),
                jnp.where(lane % 32 == 31, pick(z_high, spread), turned(own[j], 127)),
            )
        )
    return own, result


def parity():
    lane = lanes()
    return (sublanes() + lane // 32 + lane) % 2


def prepare_kernel(scalars, v, f, k, c, kind, v2, f2, k2, c2, kind2, wv, wf, wk, wc, wa, faces):
    core, base, extra = whereabouts(scalars)
    first, middle, last = scalars[0], scalars[1], scalars[2]
    held = jnp.where(core == 0, middle - first, last - middle)

    def opened(kinds):
        return 1.0 - 0.5 * kinds.astype(F32)

    def copy(source, s, other):
        if other:
            wv[s], wf[s], wk[s], wc[s] = v2[source], f2[source], k2[source], c2[source]
            wa[s] = opened(kind2[source])
        else:
            wv[s], wf[s], wk[s], wc[s] = v[source], f[source], k[source], c[source]
            wa[s] = opened(kind[source])

    def one(s, carry):
        inside = jnp.where(core == 0, s < held, s >= 4 - held)
        mine = jnp.where(core == 0, s, s + held - 4)
        theirs = jnp.where(core == 0, s - held, s + held - 2)

        @pl.when(inside)
        def _():
            copy(mine, s, False)

        @pl.when(jnp.logical_not(inside))
        def _():
            copy(theirs, s, True)

        ix, iy, _ = place(base, s)
        for number, ref in enumerate((wv, wk, wa)):
            part = faces.at[pl.ds(4 * number, 4)]
            for xt in range(TILES):
                tiles = [tile_at(ref.at[s], xt, j) for j in range(COLS)]
                extract(s, xt, tiles, iy, part)
            for j in range(COLS):
                extract_row(s, j, tile_at(ref.at[s], 0, j), tile_at(ref.at[s], 3, j), ix, part)
        return carry

    lax.fori_loop(0, SLOTS, one, 0)


def first_kernel(layers, scalars, v, f, k, c, a, own, oth, far, post, vo, fo, do, go, faces, ghost, pads):
    where = whereabouts(scalars)
    base = where[1]
    for number in range(3):
        part = pl.ds(4 * number, 4)
        ghosts(where, own.at[part], oth.at[part], far.at[part], post.at[part], ghost.at[number])

    def one(s, carry):
        ix, iy, iz = place(base, s)
        for number, ref in enumerate((v, k, a)):
            pad(s, ref, ghost.at[number], pads.at[number])
        lane, row = lanes(), sublanes()
        shade = parity()
        for xt in range(TILES):
            rows = pl.ds(8 * xt, 8)
            vs, vn = around(s, xt, pads.at[0], ghost.at[0])
            ks, kn = around(s, xt, pads.at[1], ghost.at[1])
            aps, an = around(s, xt, pads.at[2], ghost.at[2])
            fresh = []
            for j in range(COLS):
                cols = pl.ds(128 * j, 128)
                outside = [None] * 6
                if xt == 0:
                    outside[0] = (row == 0) & (ix == 0)
                if xt == TILES - 1:
                    outside[1] = (row == 7) & (ix == 1)
                if j == 0:
                    outside[2] = (lane < 32) & (iy == 0)
                if j == COLS - 1:
                    outside[3] = (lane >= 96) & (iy == 1)
                outside[4] = (lane % 32 == 0) & (iz == 0)
                outside[5] = (lane % 32 == 31) & (iz == layers - 1)
                heat, opening = ks[j], aps[j]
                coefficients = []
                summed = None
                for way in range(6):
                    heat2, opening2 = kn[j][way], an[j][way]
                    if outside[way] is not None:
                        heat2 = jnp.where(outside[way], heat, heat2)
                        opening2 = jnp.where(outside[way], 1.0, opening2)
                    b = opening * opening2 * (2.0 * heat * heat2) / (heat + heat2)
                    summed = b if summed is None else summed + b
                    if outside[way] is not None:
                        b = jnp.where(outside[way], 0.0, b)
                    coefficients.append(b)
                diagonal = jnp.where(
                    opening == 0.0,
                    1.0,
                    c[s, rows, cols] + summed + jnp.where(opening == 0.5, heat, 0.0),
                )
                inverse = 1.0 / diagonal
                total = f[s, rows, cols] * inverse
                fo[s, rows, cols] = total
                do[s, rows, cols] = diagonal
                for way in range(6):
                    g = coefficients[way] * inverse
                    go[way, s, rows, cols] = g
                    total = total + g * vn[j][way]
                new = jnp.where(shade == 0, total, vs[j])
                vo[s, rows, cols] = new
                fresh.append(new)
            extract(s, xt, fresh, iy, faces)
        for j in range(COLS):
            extract_row(s, j, tile_at(vo.at[s], 0, j), tile_at(vo.at[s], 3, j), ix, faces)
        return carry

    lax.fori_loop(0, SLOTS, one, 0)


def sweep_kernel(shade_now, scalars, v, f, g, own, oth, far, post, vo, faces, ghost, padded):
    where = whereabouts(scalars)
    base = where[1]
    ghosts(where, own, oth, far, post, ghost)

    def one(s, carry):
        ix, iy, _ = place(base, s)
        pad(s, v, ghost, padded)
        shade = parity()
        for xt in range(TILES):
            rows = pl.ds(8 * xt, 8)
            mine, near = around(s, xt, padded, ghost)
            fresh = []
            for j in range(COLS):
                cols = pl.ds(128 * j, 128)
                total = f[s, rows, cols]
                for way in range(6):
                    total = total + g[way, s, rows, cols] * near[j][way]
                new = jnp.where(shade == shade_now, total, mine[j])
                vo[s, rows, cols] = new
                fresh.append(new)
            extract(s, xt, fresh, iy, faces)
        for j in range(COLS):
            extract_row(s, j, tile_at(vo.at[s], 0, j), tile_at(vo.at[s], 3, j), ix, faces)
        return carry

    lax.fori_loop(0, SLOTS, one, 0)


def residual_kernel(scalars, v, f, g, d, own, oth, far, post, level, blocks, ghost, padded, rest):
    where = whereabouts(scalars)
    core = where[0]
    first, middle, last = scalars[0], scalars[1], scalars[2]
    held = jnp.where(core == 0, middle - first, last - middle)
    ghosts(where, own, oth, far, post, ghost)

    def one(s, carry):
        pad(s, v, ghost, padded)
        for xt in range(TILES):
            rows = pl.ds(8 * xt, 8)
            mine, near = around(s, xt, padded, ghost)
            for j in range(COLS):
                cols = pl.ds(128 * j, 128)
                total = f[s, rows, cols]
                for way in range(6):
                    total = total + g[way, s, rows, cols] * near[j][way]
                rest[j, rows, :] = d[s, rows, cols] * (total - mine[j])
        lane = lax.broadcasted_iota(jnp.int32, (8, 128), 1)
        index = 64 * ((lane // 16) % 2) + 2 * (lane % 16)
        for xt in range(2):
            for t in range(2):
                found = None
                for q in range(4):
                    j = 4 * t + q
                    pair = rest[j, pl.ds(16 * xt, 8, stride=2), :] + rest[j, pl.ds(16 * xt + 1, 8, stride=2), :]
                    pair = pair + turned(pair, 127)
                    pair = pair + turned(pair, 96)
                    pair = pick(pair, index)
                    found = pair if found is None else jnp.where(lane // 32 == q, pair, found)
                blocks[s, pl.ds(8 * xt, 8), pl.ds(128 * t, 128)] = found * 0.125
        filled = s < held

        @pl.when(filled)
        def _():
            level[s] = v[jnp.where(core == 0, s, 4 - held + s)]

        @pl.when(jnp.logical_not(filled))
        def _():
            level[s] = jnp.zeros((SPAN, LAYER), F32)

        return carry

    lax.fori_loop(0, SLOTS, one, 0)


def coarse_kernel(scalars, own, far, post, grid, table):
    core = scalars[4]
    first, middle, last, next_last, total = scalars[0], scalars[1], scalars[2], scalars[3], scalars[5]
    mine = jnp.where(core == 0, first, middle)
    mine_end = jnp.where(core == 0, middle, last)
    leader = lax.div(mine + 7, 8) * 8
    held = leader < mine_end
    low = core == 0
    for i in range(4):
        j = 4 + i
        table[i] = jnp.where(low, own[i], own[j])
        table[j] = jnp.where(low, own[j], own[i])
        table[8 + i] = jnp.where(low, post[i], far[i])
        table[12 + i] = jnp.where(low, post[j], far[j])
        table[16 + i] = jnp.where(low, far[j], post[j])

    def source(patch):
        here = patch - first
        there = patch - last
        beyond = patch - next_last
        entry = jnp.where(here < 4, here, here - (last - first - 4) + 4)
        entry2 = 8 + jnp.where(there < 4, there, there - (next_last - last - 4) + 4)
        entry3 = 16 + beyond
        found = jnp.where(patch < last, entry, jnp.where(patch < next_last, entry2, entry3))
        return jnp.clip(found, 0, 19)

    lane = lanes()

    @pl.when(held)
    def _():
        for ix in range(2):
            for iy in range(2):
                under = source(leader + ix + 2 * iy)
                over = source(leader + ix + 2 * iy + 4)
                for xt in range(2):
                    for jj in range(4):
                        index = 16 * (4 * (jj % 2) + lane // 32) + lane % 16
                        cols = pl.ds(128 * (jj // 2), 128)
                        rows = pl.ds(8 * xt, 8)
                        a = pick(table[under, rows, cols], index)
                        b = pick(table[over, rows, cols], index)
                        grid[0, pl.ds(16 * ix + 8 * xt, 8), pl.ds(512 * iy + 128 * jj, 128)] = jnp.where(
                            lane % 32 < 16, a, b
                        )

    @pl.when(jnp.logical_not(held))
    def _():
        grid[0] = jnp.zeros((SPAN, LAYER), F32)


def call(kernel, out_shape, operands, scratch=(), name=None):
    return pl.pallas_call(
        kernel,
        out_shape=out_shape,
        in_specs=[SMEM] + [VMEM] * (len(operands) - 1),
        out_specs=jax.tree.map(lambda _: VMEM, out_shape),
        scratch_shapes=list(scratch),
        compiler_params=pltpu.CompilerParams(vmem_limit_bytes=32 * 1024 * 1024),
        name=name,
    )(*operands)


def shards(v, f, k, c, kind, holder):
    devices = lax.axis_size(AXES)
    device = lax.axis_index(AXES)
    core = lax.rem(device, 2)
    chip = device - core
    swap = [(i, i ^ 1) for i in range(devices)]
    reach = [(i, i + 1) for i in range(1, devices - 1, 2)]
    reach = reach + [(b, a) for a, b in reach]
    patches = holder.shape[0]

    bounds = chip + jnp.array([0, 1, 2, 4], jnp.int32)
    starts = jnp.sum((holder[None, :] < bounds[:, None]).astype(jnp.int32), axis=1)
    scalars = jnp.concatenate([starts, jnp.stack([core, jnp.int32(patches)])])

    def exchange(faces):
        far = lax.ppermute(faces, AXES, reach)
        oth = lax.ppermute(faces, AXES, swap)
        post = lax.ppermute(far, AXES, swap)
        return faces, oth, far, post

    lend = jnp.where(core == 0, starts[1] - starts[0] - 2, 0)
    borrowed = [
        lax.ppermute(lax.dynamic_slice_in_dim(x, lend, 2, 0), AXES, swap) for x in (v, f, k, c, kind)
    ]
    three = jax.ShapeDtypeStruct((12, SPAN, 128), F32)
    wv, wf, wk, wc, wa, faces = call(
        prepare_kernel, [FIELD] * 5 + [three], [scalars, v, f, k, c, kind, *borrowed], name="prepare"
    )
    coefficients = jax.ShapeDtypeStruct((6, SLOTS, SPAN, LAYER), F32)
    wv, wf, wd, wg, faces = call(
        functools.partial(first_kernel, patches // 4),
        [FIELD, FIELD, FIELD, coefficients, FACES],
        [scalars, wv, wf, wk, wc, wa, *exchange(faces)],
        [pltpu.VMEM((3, 4, SPAN, 128), F32), pltpu.VMEM((3, 48, LAYER), F32)],
        name="first",
    )
    ghost_scratch = [pltpu.VMEM((4, SPAN, 128), F32), pltpu.VMEM((48, LAYER), F32)]
    for shade in (1, 0, 1):
        wv, faces = call(
            functools.partial(sweep_kernel, shade),
            [FIELD, FACES],
            [scalars, wv, wf, wg, *exchange(faces)],
            ghost_scratch,
            name="sweep",
        )
    block_shape = jax.ShapeDtypeStruct((SLOTS, SPAN // 2, 256), F32)
    level, blocks = call(
        residual_kernel,
        [FIELD, block_shape],
        [scalars, wv, wf, wg, wd, *exchange(faces)],
        ghost_scratch + [pltpu.VMEM((COLS, SPAN, 128), F32)],
        name="residual",
    )
    both = jnp.concatenate([blocks, lax.ppermute(blocks, AXES, swap)], 0)
    downward = [(i, i - 1) for i in range(2, devices, 2)] + [(i, i - 5) for i in range(5, devices, 2)]
    far = lax.ppermute(both, AXES, downward)
    post = lax.ppermute(far, AXES, swap)
    grid = call(
        coarse_kernel,
        jax.ShapeDtypeStruct((1, SPAN, LAYER), F32),
        [scalars, both, far, post],
        [pltpu.VMEM((20, SPAN // 2, 256), F32)],
        name="coarse",
    )
    return level, grid


def solution(mesh):
    spec = P(AXES, None, None)
    return jax.shard_map(
        shards,
        mesh=mesh,
        in_specs=(spec, spec, spec, spec, spec, P()),
        out_specs=(spec, spec),
        check_vma=False,
    )
```

```python
import functools

import jax
import jax.numpy as jnp
from jax import lax
from jax.experimental import pallas as pl
from jax.experimental.pallas import tpu as pltpu
from jax.sharding import PartitionSpec as P

COLLECT_LIMIT = 56
AXES = ("wide", "narrow")
SPAN = 32
LAYER = 1024
SLOTS = 4
TILES = 4
F32 = jnp.float32
VMEM = pl.BlockSpec(memory_space=pltpu.VMEM)
SMEM = pl.BlockSpec(memory_space=pltpu.SMEM)
HBM = pl.BlockSpec(memory_space=pl.ANY)
FACES = jax.ShapeDtypeStruct((4, SPAN, 128), F32)
FIELD = jax.ShapeDtypeStruct((LAYER, 128), F32)
GHOSTS = pltpu.VMEM((4, SPAN, 128), F32)
PADDED = pltpu.VMEM((SPAN + 2, 48, 128), F32)


def lanes():
    return lax.broadcasted_iota(jnp.int32, (8, 128), 1)


def pick(tile, index):
    return jnp.take_along_axis(tile, index, axis=1, mode="promise_in_bounds")


def turned(tile, by):
    return pltpu.roll(tile, by, axis=1)


def part(xt):
    return pl.ds(8 * xt, 8)


def tile_row(y, zt):
    return pl.ds(pl.multiple_of(SPAN * y + 8 * zt, 8), 8)


def whereabouts(scalars):
    core = scalars[4]
    first, last = scalars[0], scalars[2]
    return core, jnp.where(core == 0, first, last - 4), last - first - 4


def positions(base):
    patch = base + lanes() // 32
    return patch % 2, (patch // 2) % 2, patch // 4


def put_faces(base, ref, faces):
    ix, iy, _ = positions(base)
    lane = lanes()
    for t in range(TILES):
        faces[0, part(t), :] = ref[pl.ds(256 * t, 8, stride=SPAN), :]
        faces[1, part(t), :] = ref[pl.ds(256 * t + 31, 8, stride=SPAN), :]
        faces[2, part(t), :] = jnp.where(iy == 1, ref[part(t), :], ref[pl.ds(31 * SPAN + 8 * t, 8), :])
    index = 32 * (lane // 32) + jnp.where(ix == 1, 0, 31)
    for t in range(TILES):
        found = pick(ref[part(t), :], index)
        for y in range(1, SPAN):
            found = jnp.where(lane % 32 == y, pick(ref[pl.ds(SPAN * y + 8 * t, 8), :], index), found)
        faces[3, part(t), :] = found


def ghosts(where, own, oth, far, post, out):
    core, base, extra = where
    lane = lanes()
    ix, iy, _ = positions(base)
    low = core == 0
    start = jnp.where(low, 4 - extra, extra)
    moved = (lane + 32 * start) % 128
    cut = 128 - 32 * start

    def window(face, slab, rows):
        a, b = oth[face, rows, :], post[slab, rows, :]
        lead = pick(jnp.where(low, a, b), moved)
        tail = pick(jnp.where(low, b, a), moved)
        return jnp.where(lane < cut, lead, tail)

    def sides(face, slab, rows):
        mid = window(face, slab, rows)
        edge = far[slab, rows, :]
        return jnp.where(low, edge, mid), jnp.where(low, mid, edge)

    for t in range(TILES):
        rows = part(t)
        out[0, rows, :], out[1, rows, :] = sides(core, 0, rows)
        below, above = sides(2, 1, rows)
        inner = turned(own[2, rows, :], 64)
        out[2, rows, :] = jnp.where(
            iy == 1,
            jnp.where(lane < 64, turned(below, 64), inner),
            jnp.where(lane < 64, inner, turned(above, 64)),
        )
        below, above = sides(3, 2, rows)
        inner = own[3, rows, :]
        out[3, rows, :] = jnp.where(
            ix == 1,
            turned(jnp.where(lane < 96, inner, below), 32),
            turned(jnp.where(lane < 32, above, inner), 96),
        )


def pad(base, ref, ghost, padded, outside):
    _, iy, iz = positions(base)
    for t in range(TILES):
        rows = part(t)
        low_own, high_own = ref[rows, :], ref[pl.ds(31 * SPAN + 8 * t, 8), :]
        padded[0, 8 + 8 * t : 16 + 8 * t, :] = jnp.where(iy == 1, ghost[2, rows, :], outside(low_own))
        padded[SPAN + 1, 8 + 8 * t : 16 + 8 * t, :] = jnp.where(iy == 0, ghost[2, rows, :], outside(high_own))

    def layer(y, carry):
        for t in range(TILES):
            padded[y + 1, 8 + 8 * t : 16 + 8 * t, :] = ref[tile_row(y, t), :]
        padded[y + 1, 7:8, :] = ghost[0, pl.ds(y, 1), :]
        padded[y + 1, 40:41, :] = ghost[1, pl.ds(y, 1), :]
        return carry

    lax.fori_loop(0, SPAN, layer, 0, unroll=4)


def around(y, t, padded, ghost):
    lane = lanes()
    rows = slice(8 + 8 * t, 16 + 8 * t)
    own = padded[y + 1, rows, :]
    beyond = pick(ghost[3, part(t), :], 32 * (lane // 32) + y)
    return own, (
        jnp.where(lane % 32 == 0, beyond, turned(own, 1)),
        jnp.where(lane % 32 == 31, beyond, turned(own, 127)),
        padded[y, rows, :],
        padded[y + 2, rows, :],
        padded[y + 1, 7 + 8 * t : 15 + 8 * t, :],
        padded[y + 1, 9 + 8 * t : 17 + 8 * t, :],
    )


def parity(y):
    return (lax.broadcasted_iota(jnp.int32, (8, 128), 0) + lanes() + y) % 2


def inverted(x):
    guess = pl.reciprocal(x, approx=True)
    return guess * (2.0 - x * guess)


def zero(own):
    return 0.0


def collect_kernel(holder, v, f, k, c, kind, scalars, own, faces, bounds, hv, hf, hk, hc, hkind, sems):
    device = lax.axis_index(AXES)
    core = lax.rem(device, 2)
    source = (v, f, k, c, kind)
    landed = (hv, hf, hk, hc, hkind)
    copies = [pltpu.make_async_copy(source[i], landed[i], sems.at[i]) for i in range(5)]
    counting = pltpu.make_async_copy(holder, bounds, sems.at[5])
    order = (0, 2, 4, 1, 3)
    counting.start()
    for i in order:
        copies[i].start()
    counting.wait()
    count = []
    for bound in (0, 1, 2, 4):
        count.append(jnp.sum((bounds[...] < device - core + bound).astype(jnp.int32)))
        scalars[len(count) - 1] = count[-1]
    scalars[4] = core
    base = jnp.where(core == 0, count[0], count[1])
    for i in order:
        copies[i].wait()
        for j in range(8):
            block = landed[i][:, pl.ds(128 * j, 128)].T
            if i == 4:
                block = 1.0 - 0.5 * block.astype(F32)
            own[i, pl.ds(128 * j, 128), :] = block
        if i in (0, 2, 4):
            put_faces(base, own.at[i], faces.at[pl.ds(2 * i, 4)])


def window_of(scalars):
    core, extra = scalars[4], scalars[2] - scalars[0] - 4
    held = jnp.where(core == 0, scalars[1] - scalars[0], scalars[2] - scalars[1])
    lane = lanes()
    low = core == 0
    index = (lane + jnp.where(low, 0, 32 * held)) % 128
    index_other = (lane + jnp.where(low, 128 - 32 * held, 32 * extra)) % 128
    inside = (lane >= jnp.where(low, 0, 128 - 32 * held)) & (lane < jnp.where(low, 32 * held, 128))
    return lambda own, oth: jnp.where(inside, pick(own, index), pick(oth, index_other))


def face_window_kernel(scalars, own, oth, faces, sent):
    windowed = window_of(scalars)
    for i in range(12):
        for t in range(TILES):
            faces[i, part(t), :] = windowed(own[i, part(t), :], oth[i, part(t), :])
    for i in range(3):
        put_sent(scalars, faces.at[pl.ds(4 * i, 4)], sent.at[pl.ds(3 * i, 3)])


def put_sent(scalars, faces, sent):
    for t in range(TILES):
        sent[0, part(t), :] = faces[scalars[4], part(t), :]
        sent[1, part(t), :] = faces[2, part(t), :]
        sent[2, part(t), :] = faces[3, part(t), :]


def window_kernel(scalars, own, oth, window):
    windowed = window_of(scalars)
    for i in range(5):

        def rows(y, carry):
            for t in range(TILES):
                at = tile_row(y, t)
                window[i, at, :] = windowed(own[i, at, :], oth[i, at, :])
            return carry

        lax.fori_loop(0, SPAN, rows, 0, unroll=8)


def first_kernel(layers, scalars, fields, own, oth, far, post, vo, fo, do, go, faces, sent, ghost, pv, pk, pa):
    v, f, k, c, a = (fields.at[i] for i in range(5))
    where = whereabouts(scalars)
    base = where[1]
    ix, iy, iz = positions(base)
    lane = lanes()
    for number in range(3):
        group, outer = pl.ds(4 * number, 4), pl.ds(3 * number, 3)
        ghosts(where, own.at[group], oth.at[group], far.at[outer], post.at[outer], ghost.at[number])
    for t in range(TILES):
        rows = part(t)
        for face, gone, row in ((0, iz == 0, 0), (1, iz == layers - 1, 31)):
            edge = k[pl.ds(256 * t + row, 8, stride=SPAN), :]
            ghost[1, face, rows, :] = jnp.where(gone, edge, ghost[1, face, rows, :])
            ghost[2, face, rows, :] = jnp.where(gone, 1.0, ghost[2, face, rows, :])
    pad(base, v, ghost.at[0], pv, zero)
    pad(base, k, ghost.at[1], pk, lambda mine: mine)
    pad(base, a, ghost.at[2], pa, lambda mine: 1.0)
    edges = ((lane % 32 == 0) & (ix == 0), (lane % 32 == 31) & (ix == 1))

    def layer(y, carry):
        shade = parity(y)
        for t in range(TILES):
            rows = tile_row(y, t)
            value, values = around(y, t, pv, ghost.at[0])
            heat, heats = around(y, t, pk, ghost.at[1])
            opening, openings = around(y, t, pa, ghost.at[2])
            coefficients = []
            summed = None
            doubled = 2.0 * opening * heat
            for way in range(6):
                heat2, opening2 = heats[way], openings[way]
                if way < 2:
                    heat2 = jnp.where(edges[way], heat, heat2)
                    opening2 = jnp.where(edges[way], 1.0, opening2)
                b = doubled * opening2 * heat2 * inverted(heat + heat2)
                summed = b if summed is None else summed + b
                coefficients.append(jnp.where(edges[way], 0.0, b) if way < 2 else b)
            wall = jnp.where(opening == 0.5, heat, 0.0)
            diagonal = jnp.where(opening == 0.0, 1.0, c[rows, :] + summed + wall)
            inverse = inverted(diagonal)
            total = f[rows, :] * inverse
            fo[rows, :] = total
            do[rows, :] = diagonal
            for way in range(6):
                g = coefficients[way] * inverse
                go[way, rows, :] = g
                total = total + g * values[way]
            vo[rows, :] = jnp.where(shade == 0, total, value)
        return carry

    lax.fori_loop(0, SPAN, layer, 0, unroll=4)
    put_faces(base, vo, faces)
    put_sent(scalars, faces, sent)


def relaxed(y, t, f, g, padded, ghost):
    rows = tile_row(y, t)
    value, values = around(y, t, padded, ghost)
    total = f[rows, :]
    for way in range(6):
        total = total + g[way, rows, :] * values[way]
    return value, total


def sweep_kernel(shade_now, scalars, v, f, g, own, oth, far, post, vo, faces, sent, ghost, padded):
    where = whereabouts(scalars)
    base = where[1]
    ghosts(where, own, oth, far, post, ghost)
    pad(base, v, ghost, padded, zero)

    def layer(y, carry):
        shade = parity(y)
        for t in range(TILES):
            value, total = relaxed(y, t, f, g, padded, ghost)
            vo[tile_row(y, t), :] = jnp.where(shade == shade_now, total, value)
        return carry

    lax.fori_loop(0, SPAN, layer, 0, unroll=8)
    put_faces(base, vo, faces)
    put_sent(scalars, faces, sent)


def residual_kernel(scalars, v, f, g, d, own, oth, far, post, blocks, ghost, padded, pair):
    where = whereabouts(scalars)
    ghosts(where, own, oth, far, post, ghost)
    pad(where[1], v, ghost, padded, zero)
    lane = lanes()
    index = 2 * (lane % 64)

    def layer(y4, carry):
        for half in range(2):
            for t in range(TILES):
                added = None
                for step in range(2):
                    y = 4 * y4 + 2 * half + step
                    value, total = relaxed(y, t, f, g, padded, ghost)
                    rest = d[tile_row(y, t), :] * (total - value)
                    added = rest if added is None else added + rest
                pair[half, part(t), :] = added + turned(added, 127)
        for t in range(2):
            both = []
            for half in range(2):
                even = pair[half, pl.ds(16 * t, 8, stride=2), :]
                odd = pair[half, pl.ds(16 * t + 1, 8, stride=2), :]
                both.append(pick(even + odd, index))
            blocks[pl.ds(pl.multiple_of(16 * y4 + 8 * t, 8), 8), :] = (
                jnp.where(lane < 64, both[0], both[1]) * 0.125
            )
        return carry

    lax.fori_loop(0, 8, layer, 0, unroll=2)


def level_kernel(scalars, v, level, stack):
    core = scalars[4]
    held = jnp.where(core == 0, scalars[1] - scalars[0], scalars[2] - scalars[1])
    for j in range(8):
        stack[:, pl.ds(128 * j, 128)] = v[pl.ds(128 * j, 128), :].T
    for s in range(SLOTS):
        filled = s < held
        source = jnp.where(core == 0, s, jnp.where(filled, 4 - held + s, 0))
        for t in range(TILES):
            rows = pl.ds(pl.multiple_of(32 * source + 8 * t, 8), 8)
            level[s, part(t), :] = jnp.where(filled, stack[rows, :], 0.0)


def coarse_kernel(scalars, own, far, post, grid, table, joined):
    core = scalars[4]
    first, middle, last, next_last = scalars[0], scalars[1], scalars[2], scalars[3]
    mine = jnp.where(core == 0, first, middle)
    mine_end = jnp.where(core == 0, middle, last)
    leader = lax.div(mine + 7, 8) * 8
    held = leader < mine_end
    low = core == 0
    lane = lanes()

    @pl.when(held)
    def _():
        for t in range(16):
            rows = part(t)
            table[0, rows, :] = jnp.where(low, own[0, rows, :], own[1, rows, :])
            table[1, rows, :] = jnp.where(low, own[1, rows, :], own[0, rows, :])
            table[2, rows, :] = jnp.where(low, post[0, rows, :], far[0, rows, :])
            table[3, rows, :] = jnp.where(low, post[1, rows, :], far[1, rows, :])
            table[4, rows, :] = jnp.where(low, far[1, rows, :], post[1, rows, :])

        def source(patch):
            here = patch - first
            there = patch - last
            extra, extra2 = last - first - 4, next_last - last - 4
            entry = jnp.where(here < 4, here, here - extra + 4)
            entry2 = 8 + jnp.where(there < 4, there, there - extra2 + 4)
            entry3 = 16 + patch - next_last
            found = jnp.where(patch < last, entry, jnp.where(patch < next_last, entry2, entry3))
            found = jnp.clip(found, 0, 19)
            return lax.div(found, 4), lax.rem(found, 4)

        for iy in range(2):
            for iz in range(2):
                left, left_slot = source(leader + 2 * iy + 4 * iz)
                right, right_slot = source(leader + 1 + 2 * iy + 4 * iz)
                for y in range(16):
                    for t in range(2):
                        rows = pl.ds(16 * (y // 2) + 8 * t, 8)
                        index = 64 * (y % 2) + lane % 16
                        a = pick(table[left, rows, :], index + 16 * left_slot)
                        b = pick(table[right, rows, :], index + 16 * right_slot)
                        joined[pl.ds(SPAN * (16 * iy + y) + 16 * iz + 8 * t, 8), :] = jnp.where(lane < 16, a, b)
        for j in range(8):
            turn = joined[pl.ds(128 * j, 128), :].T
            grid[0, :, pl.ds(128 * j, 128)] = turn[0:SPAN, :]

    @pl.when(jnp.logical_not(held))
    def _():
        grid[0] = jnp.zeros((SPAN, LAYER), F32)


def call(kernel, out_shape, operands, specs=None, out_specs=None, scratch=(), name=None, limit=32, leading=(SMEM,)):
    return pl.pallas_call(
        kernel,
        out_shape=out_shape,
        in_specs=list(leading) + (specs or [VMEM] * (len(operands) - 1)),
        out_specs=out_specs or jax.tree.map(lambda _: VMEM, out_shape),
        scratch_shapes=list(scratch),
        compiler_params=pltpu.CompilerParams(vmem_limit_bytes=limit * 1024 * 1024),
        name=name,
    )(*operands)


def shards(v, f, k, c, kind, holder):
    devices = lax.axis_size(AXES)
    swap = [(i, i ^ 1) for i in range(devices)]
    reach = [(i, i + 1) for i in range(1, devices - 1, 2)]
    reach = reach + [(b, a) for a, b in reach]
    patches = holder.shape[0]

    def exchange(faces, sent):
        far = lax.ppermute(sent, AXES, reach)
        oth = lax.ppermute(faces, AXES, swap)
        post = lax.ppermute(far, AXES, swap)
        return faces, oth, far, post

    fields = [x.reshape(SLOTS * SPAN, LAYER) for x in (v, f, k, c, kind)]
    five = jax.ShapeDtypeStruct((5, LAYER, 128), F32)
    twelve = jax.ShapeDtypeStruct((12, SPAN, 128), F32)
    nine = jax.ShapeDtypeStruct((9, SPAN, 128), F32)
    three = jax.ShapeDtypeStruct((3, SPAN, 128), F32)
    scalars, own, faces = call(
        collect_kernel,
        [pltpu.SMEM((5,), jnp.int32), pltpu.VMEM(five.shape, F32), pltpu.VMEM(twelve.shape, F32)],
        [holder.reshape(patches // 128, 128), *fields],
        specs=[HBM] * 6,
        leading=[],
        out_specs=[SMEM, VMEM, VMEM],
        scratch=[pltpu.VMEM((patches // 128, 128), jnp.int32)]
        + [pltpu.VMEM(x.shape, x.dtype) for x in fields]
        + [pltpu.SemaphoreType.DMA((6,))],
        name="collect",
        limit=COLLECT_LIMIT,
    )
    faces, sent = call(
        face_window_kernel,
        [twelve, nine],
        [scalars, faces, lax.ppermute(faces, AXES, swap)],
        name="face_window",
    )
    sent, own = lax.optimization_barrier((sent, own))
    far = lax.ppermute(sent, AXES, reach)
    oth = lax.ppermute(faces, AXES, swap)
    window = call(window_kernel, five, [scalars, own, lax.ppermute(own, AXES, swap)], name="window")
    far, window = lax.optimization_barrier((far, window))
    post = lax.ppermute(far, AXES, swap)
    coefficients = jax.ShapeDtypeStruct((6, LAYER, 128), F32)
    wv, wf, wd, wg, faces, sent = call(
        functools.partial(first_kernel, patches // 4),
        [FIELD, FIELD, FIELD, coefficients, FACES, three],
        [scalars, window, faces, oth, far, post],
        scratch=[pltpu.VMEM((3, 4, SPAN, 128), F32)] + [PADDED] * 3,
        name="first",
    )
    for shade in (1, 0, 1):
        wv, faces, sent = call(
            functools.partial(sweep_kernel, shade),
            [FIELD, FACES, three],
            [scalars, wv, wf, wg, *exchange(faces, sent)],
            scratch=[GHOSTS, PADDED],
            name="sweep",
        )
    far = lax.ppermute(sent, AXES, reach)
    oth = lax.ppermute(faces, AXES, swap)
    level = call(
        level_kernel,
        jax.ShapeDtypeStruct((SLOTS, SPAN, LAYER), F32),
        [scalars, wv],
        scratch=[pltpu.VMEM((128, LAYER), F32)],
        name="level",
    )
    far, level = lax.optimization_barrier((far, level))
    post = lax.ppermute(far, AXES, swap)
    blocks = call(
        residual_kernel,
        jax.ShapeDtypeStruct((128, 128), F32),
        [scalars, wv, wf, wg, wd, faces, oth, far, post],
        scratch=[GHOSTS, PADDED, pltpu.VMEM((2, SPAN, 128), F32)],
        name="residual",
    )
    both = jnp.stack([blocks, lax.ppermute(blocks, AXES, swap)], 0)
    downward = [(i, i - 1) for i in range(2, devices, 2)] + [(i, i - 5) for i in range(5, devices, 2)]
    far = lax.ppermute(both, AXES, downward)
    post = lax.ppermute(far, AXES, swap)
    grid = call(
        coarse_kernel,
        jax.ShapeDtypeStruct((1, SPAN, LAYER), F32),
        [scalars, both, far, post],
        scratch=[pltpu.VMEM((5, 128, 128), F32), pltpu.VMEM((LAYER, 128), F32)],
        name="coarse",
    )
    return level, grid


def solution(mesh):
    spec = P(AXES, None, None)
    return jax.shard_map(
        shards,
        mesh=mesh,
        in_specs=(spec, spec, spec, spec, spec, P()),
        out_specs=(spec, spec),
        check_vma=False,
    )
```

```python
import functools

import jax
import jax.numpy as jnp
from jax import lax
from jax.experimental import pallas as pl
from jax.experimental.pallas import tpu as pltpu
from jax.sharding import PartitionSpec as P

COLLECT_LIMIT = 56
AXES = ("wide", "narrow")
SPAN = 32
LAYER = 1024
SLOTS = 4
TILES = 4
F32 = jnp.float32
VMEM = pl.BlockSpec(memory_space=pltpu.VMEM)
SMEM = pl.BlockSpec(memory_space=pltpu.SMEM)
HBM = pl.BlockSpec(memory_space=pl.ANY)
FACES = jax.ShapeDtypeStruct((4, SPAN, 128), F32)
FIELD = jax.ShapeDtypeStruct((LAYER, 128), F32)
GHOSTS = pltpu.VMEM((4, SPAN, 128), F32)
PADDED = pltpu.VMEM((SPAN + 2, 48, 128), F32)


def lanes():
    return lax.broadcasted_iota(jnp.int32, (8, 128), 1)


def pick(tile, index):
    return jnp.take_along_axis(tile, index, axis=1, mode="promise_in_bounds")


def turned(tile, by):
    return pltpu.roll(tile, by, axis=1)


def part(xt):
    return pl.ds(8 * xt, 8)


def tile_row(y, zt):
    return pl.ds(pl.multiple_of(SPAN * y + 8 * zt, 8), 8)


def whereabouts(scalars):
    core = scalars[0]
    first, last = scalars[1], scalars[3]
    return core, jnp.where(core == 0, first, last - 4), last - first - 4


def positions(base):
    patch = base + lanes() // 32
    return patch % 2, (patch // 2) % 2, patch // 4


def put_faces(base, ref, faces):
    ix, iy, _ = positions(base)
    lane = lanes()
    for t in range(TILES):
        faces[0, part(t), :] = ref[pl.ds(256 * t, 8, stride=SPAN), :]
        faces[1, part(t), :] = ref[pl.ds(256 * t + 31, 8, stride=SPAN), :]
        faces[2, part(t), :] = jnp.where(iy == 1, ref[part(t), :], ref[pl.ds(31 * SPAN + 8 * t, 8), :])
    index = 32 * (lane // 32) + jnp.where(ix == 1, 0, 31)
    for t in range(TILES):
        found = pick(ref[part(t), :], index)
        for y in range(1, SPAN):
            found = jnp.where(lane % 32 == y, pick(ref[pl.ds(SPAN * y + 8 * t, 8), :], index), found)
        faces[3, part(t), :] = found


def ghosts(where, own, oth, far, post, out):
    core, base, extra = where
    lane = lanes()
    ix, iy, _ = positions(base)
    low = core == 0
    start = jnp.where(low, 4 - extra, extra)
    moved = (lane + 32 * start) % 128
    cut = 128 - 32 * start

    def window(face, slab, rows):
        a = oth[face, rows, :]
        b = jnp.zeros((8, 128), F32) if post is None else post[slab, rows, :]
        lead = pick(jnp.where(low, a, b), moved)
        tail = pick(jnp.where(low, b, a), moved)
        return jnp.where(lane < cut, lead, tail)

    def sides(face, slab, rows):
        mid = window(face, slab, rows)
        edge = jnp.zeros((8, 128), F32) if far is None else far[slab, rows, :]
        return jnp.where(low, edge, mid), jnp.where(low, mid, edge)

    for t in range(TILES):
        rows = part(t)
        out[0, rows, :], out[1, rows, :] = sides(core, 0, rows)
        below, above = sides(2, 1, rows)
        inner = turned(own[2, rows, :], 64)
        out[2, rows, :] = jnp.where(
            iy == 1,
            jnp.where(lane < 64, turned(below, 64), inner),
            jnp.where(lane < 64, inner, turned(above, 64)),
        )
        below, above = sides(3, 2, rows)
        inner = own[3, rows, :]
        out[3, rows, :] = jnp.where(
            ix == 1,
            turned(jnp.where(lane < 96, inner, below), 32),
            turned(jnp.where(lane < 32, above, inner), 96),
        )


def pad(base, ref, ghost, padded, outside):
    _, iy, iz = positions(base)
    for t in range(TILES):
        rows = part(t)
        low_own, high_own = ref[rows, :], ref[pl.ds(31 * SPAN + 8 * t, 8), :]
        padded[0, 8 + 8 * t : 16 + 8 * t, :] = jnp.where(iy == 1, ghost[2, rows, :], outside(low_own))
        padded[SPAN + 1, 8 + 8 * t : 16 + 8 * t, :] = jnp.where(iy == 0, ghost[2, rows, :], outside(high_own))

    def layer(y, carry):
        for t in range(TILES):
            padded[y + 1, 8 + 8 * t : 16 + 8 * t, :] = ref[tile_row(y, t), :]
        padded[y + 1, 7:8, :] = ghost[0, pl.ds(y, 1), :]
        padded[y + 1, 40:41, :] = ghost[1, pl.ds(y, 1), :]
        return carry

    lax.fori_loop(0, SPAN, layer, 0, unroll=4)


def around(y, t, padded, ghost):
    lane = lanes()
    rows = slice(8 + 8 * t, 16 + 8 * t)
    own = padded[y + 1, rows, :]
    beyond = pick(ghost[3, part(t), :], 32 * (lane // 32) + y)
    return own, (
        jnp.where(lane % 32 == 0, beyond, turned(own, 1)),
        jnp.where(lane % 32 == 31, beyond, turned(own, 127)),
        padded[y, rows, :],
        padded[y + 2, rows, :],
        padded[y + 1, 7 + 8 * t : 15 + 8 * t, :],
        padded[y + 1, 9 + 8 * t : 17 + 8 * t, :],
    )


def parity(y):
    return (lax.broadcasted_iota(jnp.int32, (8, 128), 0) + lanes() + y) % 2


def inverted(x):
    guess = pl.reciprocal(x, approx=True)
    return guess * (2.0 - x * guess)


def zero(own):
    return 0.0


def collect_kernel(holder, v, f, k, c, kind, scalars, own, faces, bounds, hv, hf, hk, hc, hkind, sems):
    device = lax.axis_index(AXES)
    core = lax.rem(device, 2)
    source = (v, f, k, c, kind)
    landed = (hv, hf, hk, hc, hkind)
    copies = [pltpu.make_async_copy(source[i], landed[i], sems.at[i]) for i in range(5)]
    counting = pltpu.make_async_copy(holder, bounds, sems.at[5])
    order = (0, 2, 4, 1, 3)
    counting.start()
    for i in order:
        copies[i].start()
    counting.wait()
    count = []
    for bound in (0, 1, 2, 4, 6):
        count.append(jnp.sum((bounds[...] < device - core + bound).astype(jnp.int32)))
        scalars[len(count)] = count[-1]
    scalars[0] = core
    base = jnp.where(core == 0, count[0], count[1])
    for i in order:
        copies[i].wait()
        for j in range(8):
            block = landed[i][:, pl.ds(128 * j, 128)].T
            if i == 4:
                block = 1.0 - 0.5 * block.astype(F32)
            own[i, pl.ds(128 * j, 128), :] = block
        if i in (0, 2, 4):
            put_faces(base, own.at[i], faces.at[pl.ds(2 * i, 4)])


def window_of(scalars):
    core, extra = scalars[0], scalars[3] - scalars[1] - 4
    held = jnp.where(core == 0, scalars[2] - scalars[1], scalars[3] - scalars[2])
    lane = lanes()
    low = core == 0
    index = (lane + jnp.where(low, 0, 32 * held)) % 128
    index_other = (lane + jnp.where(low, 128 - 32 * held, 32 * extra)) % 128
    inside = (lane >= jnp.where(low, 0, 128 - 32 * held)) & (lane < jnp.where(low, 32 * held, 128))
    return lambda own, oth: jnp.where(inside, pick(own, index), pick(oth, index_other))


def face_window_kernel(scalars, own, oth, faces, sent):
    windowed = window_of(scalars)
    for i in range(12):
        for t in range(TILES):
            faces[i, part(t), :] = windowed(own[i, part(t), :], oth[i, part(t), :])
    for i in range(3):
        put_sent(scalars, faces.at[pl.ds(4 * i, 4)], sent.at[pl.ds(3 * i, 3)])


def put_sent(scalars, faces, sent):
    for t in range(TILES):
        sent[0, part(t), :] = faces[scalars[0], part(t), :]
        sent[1, part(t), :] = faces[2, part(t), :]
        sent[2, part(t), :] = faces[3, part(t), :]


def window_kernel(scalars, own, oth, window):
    windowed = window_of(scalars)
    for i in range(5):

        def rows(y, carry):
            for t in range(TILES):
                at = tile_row(y, t)
                window[i, at, :] = windowed(own[i, at, :], oth[i, at, :])
            return carry

        lax.fori_loop(0, SPAN, rows, 0, unroll=8)


def first_kernel(layers, scalars, fields, own, oth, far, post, vo, fo, do, go, edge, faces, sent, ghost, pv, pk, pa):
    v, f, k, c, a = (fields.at[i] for i in range(5))
    where = whereabouts(scalars)
    base = where[1]
    ix, iy, iz = positions(base)
    lane = lanes()
    for number in range(3):
        group, outer = pl.ds(4 * number, 4), pl.ds(3 * number, 3)
        ghosts(where, own.at[group], oth.at[group], far.at[outer], post.at[outer], ghost.at[number])
    for face in range(4):
        for t in range(TILES):
            rows = part(t)
            heat, heat2 = own[4 + face, rows, :], ghost[1, face, rows, :]
            opening, opening2 = own[8 + face, rows, :], ghost[2, face, rows, :]
            edge[face, rows, :] = 2.0 * opening * heat * opening2 * heat2 * inverted(heat + heat2)
    for t in range(TILES):
        rows = part(t)
        for face, gone, row in ((0, iz == 0, 0), (1, iz == layers - 1, 31)):
            edge = k[pl.ds(256 * t + row, 8, stride=SPAN), :]
            ghost[1, face, rows, :] = jnp.where(gone, edge, ghost[1, face, rows, :])
            ghost[2, face, rows, :] = jnp.where(gone, 1.0, ghost[2, face, rows, :])
    pad(base, v, ghost.at[0], pv, zero)
    pad(base, k, ghost.at[1], pk, lambda mine: mine)
    pad(base, a, ghost.at[2], pa, lambda mine: 1.0)
    edges = ((lane % 32 == 0) & (ix == 0), (lane % 32 == 31) & (ix == 1))

    def layer(y, carry):
        shade = parity(y)
        for t in range(TILES):
            rows = tile_row(y, t)
            value, values = around(y, t, pv, ghost.at[0])
            heat, heats = around(y, t, pk, ghost.at[1])
            opening, openings = around(y, t, pa, ghost.at[2])
            coefficients = []
            summed = None
            doubled = 2.0 * opening * heat
            for way in range(6):
                heat2, opening2 = heats[way], openings[way]
                if way < 2:
                    heat2 = jnp.where(edges[way], heat, heat2)
                    opening2 = jnp.where(edges[way], 1.0, opening2)
                b = doubled * opening2 * heat2 * inverted(heat + heat2)
                summed = b if summed is None else summed + b
                coefficients.append(jnp.where(edges[way], 0.0, b) if way < 2 else b)
            wall = jnp.where(opening == 0.5, heat, 0.0)
            diagonal = jnp.where(opening == 0.0, 1.0, c[rows, :] + summed + wall)
            inverse = inverted(diagonal)
            total = f[rows, :] * inverse
            fo[rows, :] = total
            do[rows, :] = diagonal
            for way in range(6):
                g = coefficients[way] * inverse
                go[way, rows, :] = g
                total = total + g * values[way]
            vo[rows, :] = jnp.where(shade == 0, total, value)
        return carry

    lax.fori_loop(0, SPAN, layer, 0, unroll=4)
    put_faces(base, vo, faces)
    put_sent(scalars, faces, sent)


def relaxed(y, t, f, g, padded, ghost):
    rows = tile_row(y, t)
    value, values = around(y, t, padded, ghost)
    total = f[rows, :]
    for way in range(6):
        total = total + g[way, rows, :] * values[way]
    return value, total


def sweep_kernel(shade_now, scalars, v, f, g, own, oth, far, post, vo, faces, *rest):
    *sent, ghost, padded = rest
    where = whereabouts(scalars)
    base = where[1]
    ghosts(where, own, oth, far, post, ghost)
    pad(base, v, ghost, padded, zero)

    def layer(y, carry):
        shade = parity(y)
        for t in range(TILES):
            value, total = relaxed(y, t, f, g, padded, ghost)
            vo[tile_row(y, t), :] = jnp.where(shade == shade_now, total, value)
        return carry

    lax.fori_loop(0, SPAN, layer, 0, unroll=8)
    put_faces(base, vo, faces)
    if sent:
        put_sent(scalars, faces, sent[0])


def residual_kernel(scalars, v, f, g, d, edge, own, oth, blocks, cross, ghost, padded, pair):
    where = whereabouts(scalars)
    core = where[0]
    ghosts(where, own, oth, None, None, ghost)
    pad(where[1], v, ghost, padded, zero)
    lane = lanes()
    index = 2 * (lane % 64)

    def layer(y4, carry):
        for half in range(2):
            for t in range(TILES):
                added = None
                for step in range(2):
                    y = 4 * y4 + 2 * half + step
                    value, total = relaxed(y, t, f, g, padded, ghost)
                    rest = d[tile_row(y, t), :] * (total - value)
                    added = rest if added is None else added + rest
                pair[half, part(t), :] = added + turned(added, 127)
        for t in range(2):
            both = []
            for half in range(2):
                even = pair[half, pl.ds(16 * t, 8, stride=2), :]
                odd = pair[half, pl.ds(16 * t + 1, 8, stride=2), :]
                both.append(pick(even + odd, index))
            blocks[pl.ds(pl.multiple_of(16 * y4 + 8 * t, 8), 8), :] = (
                jnp.where(lane < 64, both[0], both[1]) * 0.125
            )
        return carry

    lax.fori_loop(0, 8, layer, 0, unroll=2)

    def pooled(face):
        for t in range(TILES):
            product = edge[face, part(t), :] * own[face, part(t), :]
            pair[0, part(t), :] = product + turned(product, 127)
        result = []
        for t in range(2):
            both = pair[0, pl.ds(16 * t, 8, stride=2), :] + pair[0, pl.ds(16 * t + 1, 8, stride=2), :]
            result.append(pick(both, index) * 0.125)
        return result

    for t, tile in enumerate(pooled(core)):
        cross[part(t), :] = tile
    for t, (along_y, along_x) in enumerate(zip(pooled(2), pooled(3))):
        cross[part(2 + t), :] = jnp.where(lane < 64, along_y, along_x)
    blocks[128:160, :] = cross[...]


def level_kernel(scalars, v, level, stack):
    core = scalars[0]
    held = jnp.where(core == 0, scalars[2] - scalars[1], scalars[3] - scalars[2])
    for j in range(8):
        stack[:, pl.ds(128 * j, 128)] = v[pl.ds(128 * j, 128), :].T
    for s in range(SLOTS):
        filled = s < held
        source = jnp.where(core == 0, s, jnp.where(filled, 4 - held + s, 0))
        for t in range(TILES):
            rows = pl.ds(pl.multiple_of(32 * source + 8 * t, 8), 8)
            level[s, part(t), :] = jnp.where(filled, stack[rows, :], 0.0)


def coarse_kernel(scalars, own, far, post, side, side_post, grid, table, crossing, joined):
    core = scalars[0]
    starts = [scalars[i] for i in (1, 3, 4, 5)]
    mine = jnp.where(core == 0, scalars[1], scalars[2])
    mine_end = jnp.where(core == 0, scalars[2], scalars[3])
    leader = lax.div(mine + 7, 8) * 8
    held = leader < mine_end
    low = core == 0
    lane = lanes()

    def child(patch):
        chip = (patch >= starts[1]).astype(jnp.int32) + (patch >= starts[2]).astype(jnp.int32)
        begin = jnp.where(chip == 0, starts[0], jnp.where(chip == 1, starts[1], starts[2]))
        end = jnp.where(chip == 0, starts[1], jnp.where(chip == 1, starts[2], starts[3]))
        return chip, patch - begin, end - begin

    def block(chip, j, count):
        entry = jnp.where(j < 4, j, j - count + 8)
        entry = jnp.clip(8 * chip + entry, 0, 19)
        return lax.div(entry, 4), lax.rem(entry, 4)

    @pl.when(held)
    def _():
        for t in range(16):
            rows = part(t)
            table[0, rows, :] = jnp.where(low, own[0, rows, :], own[1, rows, :])
            table[1, rows, :] = jnp.where(low, own[1, rows, :], own[0, rows, :])
            table[2, rows, :] = jnp.where(low, post[0, rows, :], far[0, rows, :])
            table[3, rows, :] = jnp.where(low, post[1, rows, :], far[1, rows, :])
            table[4, rows, :] = jnp.where(low, far[1, rows, :], post[1, rows, :])
        for t in range(4):
            rows, last = part(t), part(16 + t)
            crossing[0, rows, :] = jnp.where(low, side[rows, :], side_post[rows, :])
            crossing[1, rows, :] = jnp.where(low, own[1, last, :], own[0, last, :])
            crossing[2, rows, :] = jnp.where(low, post[1, last, :], far[1, last, :])
            crossing[3, rows, :] = jnp.where(low, post[0, last, :], far[0, last, :])
            crossing[4, rows, :] = jnp.where(low, far[1, last, :], post[1, last, :])
            crossing[5, rows, :] = jnp.where(low, side_post[rows, :], side[rows, :])

        def added(entry, rows, index, valid):
            tile = pick(crossing[jnp.clip(entry, 0, 5), rows, :], jnp.clip(index, 0, 127))
            return jnp.where(valid, tile, 0.0)

        for iy in range(2):
            for iz in range(2):
                left = child(leader + 2 * iy + 4 * iz)
                right = child(leader + 1 + 2 * iy + 4 * iz)
                left_block, left_slot = block(*left)
                right_block, right_slot = block(*right)
                for y in range(16):
                    for t in range(2):
                        rows = pl.ds(16 * (y // 2) + 8 * t, 8)
                        index = 64 * (y % 2) + lane % 16
                        a = pick(table[left_block, rows, :], index + 16 * left_slot)
                        b = pick(table[right_block, rows, :], index + 16 * right_slot)
                        joined[pl.ds(SPAN * (16 * iy + y) + 16 * iz + 8 * t, 8), :] = jnp.where(lane < 16, a, b)

                def pair_of(below, shift, rows):
                    tiles = []
                    for chip, j, count in (left, right):
                        place = j if below else j - count + 4 - shift
                        valid = (place < 4 - shift) if below else (place >= 0)
                        entry = chip if below else 3 + chip
                        slot = place + shift if below else place
                        tiles.append(added(entry, rows, 16 * slot + lane % 16, valid))
                    return jnp.where(lane < 16, tiles[0], tiles[1])

                first_row = SPAN * 16 * iy + 16 * iz
                for t in range(2):
                    at = pl.ds(first_row + 8 * SPAN * t, 8, stride=SPAN)
                    joined[at, :] = joined[at, :] + pair_of(True, 0, part(t))
                    at = pl.ds(first_row + 8 * SPAN * t + 15, 8, stride=SPAN)
                    joined[at, :] = joined[at, :] + pair_of(False, 0, part(t))
                    at = pl.ds(first_row + (0 if iy else 15 * SPAN) + 8 * t, 8)
                    joined[at, :] = joined[at, :] + pair_of(iy == 1, 2, part(2 + t))

                @pl.when(left[0] != right[0])
                def _():
                    for y in range(16):
                        for t in range(2):
                            at = pl.ds(first_row + SPAN * y + 8 * t, 8)
                            from_right = added(3 + left[0], part(2 + t), 0 * lane + 64 + y, True)
                            from_left = added(right[0], part(2 + t), 0 * lane + 112 + y, True)
                            side_tile = jnp.where(lane == 15, from_right, jnp.where(lane == 16, from_left, 0.0))
                            joined[at, :] = joined[at, :] + side_tile

        for j in range(8):
            turn = joined[pl.ds(128 * j, 128), :].T
            grid[0, :, pl.ds(128 * j, 128)] = turn[0:SPAN, :]

    @pl.when(jnp.logical_not(held))
    def _():
        grid[0] = jnp.zeros((SPAN, LAYER), F32)


def call(kernel, out_shape, operands, specs=None, out_specs=None, scratch=(), name=None, limit=32, leading=(SMEM,)):
    return pl.pallas_call(
        kernel,
        out_shape=out_shape,
        in_specs=list(leading) + (specs or [VMEM] * (len(operands) - 1)),
        out_specs=out_specs or jax.tree.map(lambda _: VMEM, out_shape),
        scratch_shapes=list(scratch),
        compiler_params=pltpu.CompilerParams(vmem_limit_bytes=limit * 1024 * 1024),
        name=name,
    )(*operands)


def shards(v, f, k, c, kind, holder):
    devices = lax.axis_size(AXES)
    swap = [(i, i ^ 1) for i in range(devices)]
    reach = [(i, i + 1) for i in range(1, devices - 1, 2)]
    reach = reach + [(b, a) for a, b in reach]
    patches = holder.shape[0]

    def exchange(faces, sent):
        far = lax.ppermute(sent, AXES, reach)
        oth = lax.ppermute(faces, AXES, swap)
        post = lax.ppermute(far, AXES, swap)
        return faces, oth, far, post

    fields = [x.reshape(SLOTS * SPAN, LAYER) for x in (v, f, k, c, kind)]
    five = jax.ShapeDtypeStruct((5, LAYER, 128), F32)
    twelve = jax.ShapeDtypeStruct((12, SPAN, 128), F32)
    nine = jax.ShapeDtypeStruct((9, SPAN, 128), F32)
    three = jax.ShapeDtypeStruct((3, SPAN, 128), F32)
    scalars, own, faces = call(
        collect_kernel,
        [pltpu.SMEM((6,), jnp.int32), pltpu.VMEM(five.shape, F32), pltpu.VMEM(twelve.shape, F32)],
        [holder.reshape(patches // 128, 128), *fields],
        specs=[HBM] * 6,
        leading=[],
        out_specs=[SMEM, VMEM, VMEM],
        scratch=[pltpu.VMEM((patches // 128, 128), jnp.int32)]
        + [pltpu.VMEM(x.shape, x.dtype) for x in fields]
        + [pltpu.SemaphoreType.DMA((6,))],
        name="collect",
        limit=COLLECT_LIMIT,
    )
    faces, sent = call(
        face_window_kernel,
        [twelve, nine],
        [scalars, faces, lax.ppermute(faces, AXES, swap)],
        name="face_window",
    )
    sent, own = lax.optimization_barrier((sent, own))
    far = lax.ppermute(sent, AXES, reach)
    oth = lax.ppermute(faces, AXES, swap)
    window = call(window_kernel, five, [scalars, own, lax.ppermute(own, AXES, swap)], name="window")
    far, window = lax.optimization_barrier((far, window))
    post = lax.ppermute(far, AXES, swap)
    coefficients = jax.ShapeDtypeStruct((6, LAYER, 128), F32)
    wv, wf, wd, wg, edge, faces, *sent = call(
        functools.partial(first_kernel, patches // 4),
        [FIELD, FIELD, FIELD, coefficients, FACES, FACES, three],
        [scalars, window, faces, oth, far, post],
        scratch=[pltpu.VMEM((3, 4, SPAN, 128), F32)] + [PADDED] * 3,
        name="first",
    )
    for shade, more in ((1, [three]), (0, [three]), (1, [])):
        wv, faces, *sent = call(
            functools.partial(sweep_kernel, shade),
            [FIELD, FACES] + more,
            [scalars, wv, wf, wg, *exchange(faces, *sent)],
            scratch=[GHOSTS, PADDED],
            name="sweep",
        )
    blocks, cross = call(
        residual_kernel,
        [jax.ShapeDtypeStruct((160, 128), F32), jax.ShapeDtypeStruct((SPAN, 128), F32)],
        [scalars, wv, wf, wg, wd, edge, faces, lax.ppermute(faces, AXES, swap)],
        scratch=[GHOSTS, PADDED, pltpu.VMEM((2, SPAN, 128), F32)],
        name="residual",
    )
    beside = [(i, i - 5) for i in range(6, devices, 2)] + [(i, i + 1) for i in range(1, devices - 1, 2)]
    side = lax.ppermute(cross, AXES, beside)
    both = jnp.stack([blocks, lax.ppermute(blocks, AXES, swap)], 0)
    downward = [(i, i - 1) for i in range(2, devices, 2)] + [(i, i - 5) for i in range(5, devices, 2)]
    far = lax.ppermute(both, AXES, downward)
    level = call(
        level_kernel,
        jax.ShapeDtypeStruct((SLOTS, SPAN, LAYER), F32),
        [scalars, wv],
        scratch=[pltpu.VMEM((128, LAYER), F32)],
        name="level",
    )
    far, side, level = lax.optimization_barrier((far, side, level))
    post = lax.ppermute(far, AXES, swap)
    side_post = lax.ppermute(side, AXES, swap)
    grid = call(
        coarse_kernel,
        jax.ShapeDtypeStruct((1, SPAN, LAYER), F32),
        [scalars, both, far, post, side, side_post],
        scratch=[pltpu.VMEM((5, 128, 128), F32), pltpu.VMEM((6, SPAN, 128), F32), pltpu.VMEM((LAYER, 128), F32)],
        name="coarse",
    )
    return level, grid


def solution(mesh):
    spec = P(AXES, None, None)
    return jax.shard_map(
        shards,
        mesh=mesh,
        in_specs=(spec, spec, spec, spec, spec, P()),
        out_specs=(spec, spec),
        check_vma=False,
    )
```

```python
import functools

import jax
import jax.numpy as jnp
from jax import lax
from jax.experimental import pallas as pl
from jax.experimental.pallas import tpu as pltpu
from jax.sharding import PartitionSpec as P

COLLECT_LIMIT = 56
AXES = ("wide", "narrow")
SPAN = 32
LAYER = 1024
SLOTS = 4
TILES = 4
F32 = jnp.float32
VMEM = pl.BlockSpec(memory_space=pltpu.VMEM)
SMEM = pl.BlockSpec(memory_space=pltpu.SMEM)
HBM = pl.BlockSpec(memory_space=pl.ANY)
FACES = jax.ShapeDtypeStruct((4, SPAN, 128), F32)
FIELD = jax.ShapeDtypeStruct((LAYER, 128), F32)
GHOSTS = pltpu.VMEM((4, SPAN, 128), F32)
PADDED = pltpu.VMEM((SPAN + 2, 48, 128), F32)


def lanes():
    return lax.broadcasted_iota(jnp.int32, (8, 128), 1)


def pick(tile, index):
    return jnp.take_along_axis(tile, index, axis=1, mode="promise_in_bounds")


def turned(tile, by):
    return pltpu.roll(tile, by, axis=1)


def part(xt):
    return pl.ds(8 * xt, 8)


def tile_row(y, zt):
    return pl.ds(pl.multiple_of(SPAN * y + 8 * zt, 8), 8)


def whereabouts(scalars):
    core = scalars[0]
    first, last = scalars[1], scalars[3]
    return core, jnp.where(core == 0, first, last - 4), last - first - 4


def positions(base):
    patch = base + lanes() // 32
    return patch % 2, (patch // 2) % 2, patch // 4


def put_faces(base, ref, faces):
    ix, iy, _ = positions(base)
    lane = lanes()
    for t in range(TILES):
        faces[0, part(t), :] = ref[pl.ds(256 * t, 8, stride=SPAN), :]
        faces[1, part(t), :] = ref[pl.ds(256 * t + 31, 8, stride=SPAN), :]
        faces[2, part(t), :] = jnp.where(iy == 1, ref[part(t), :], ref[pl.ds(31 * SPAN + 8 * t, 8), :])
    index = 32 * (lane // 32) + jnp.where(ix == 1, 0, 31)
    for t in range(TILES):
        found = pick(ref[part(t), :], index)
        for y in range(1, SPAN):
            found = jnp.where(lane % 32 == y, pick(ref[pl.ds(SPAN * y + 8 * t, 8), :], index), found)
        faces[3, part(t), :] = found


def ghosts(where, own, oth, far, post, out):
    core, base, extra = where
    lane = lanes()
    ix, iy, _ = positions(base)
    low = core == 0
    start = jnp.where(low, 4 - extra, extra)
    single = 1 if far is not None and len(far.shape) == 2 else 0
    x_far = jnp.where(low, 32, 64) + single
    x_post = jnp.where(low, 64, 32) + single
    x_turn = jnp.where(low, 96, 32)

    def mixer(turn, lift):
        target = (lane + turn) % 128
        index, index_post = (target + 32 * start) % 128, (target + 32 * start + lift) % 128
        here = jnp.where(target < 128 - 32 * start, 1, 0) == 1 - core
        if post is None:
            return lambda a, b: jnp.where(here, pick(a, index), 0.0)
        return lambda a, b: jnp.where(here, pick(a, index), pick(b, index_post))

    mix_z, mix_y, mix_x = mixer(0, 0), mixer(64, single), mixer(128 - x_turn, x_post)
    y_index = (lane + 64 + single) % 128
    x_index = (lane + x_far + jnp.where(low, 96, 32)) % 128
    own_index = jnp.where(ix == 1, lane + 96, lane + 32) % 128
    for t in range(TILES):
        rows = part(t)
        if far is None:
            z_edge = y_edge = x_edge = 0.0
            z_post = nearest_post = None
        else:
            z_edge = far[rows, :] if single else far[0, rows, :]
            nearest = z_edge if single else far[1, rows, :]
            z_post = post[rows, :] if single else post[0, rows, :]
            nearest_post = z_post if single else post[1, rows, :]
            y_edge, x_edge = pick(nearest, y_index), pick(nearest, x_index)
        mid = mix_z(oth[core, rows, :], z_post)
        out[0, rows, :], out[1, rows, :] = jnp.where(low, z_edge, mid), jnp.where(low, mid, z_edge)
        mid = mix_y(oth[2, rows, :], nearest_post)
        inner = turned(own[2, rows, :], 64)
        below, above = jnp.where(low, y_edge, mid), jnp.where(low, mid, y_edge)
        out[2, rows, :] = jnp.where(
            iy == 1, jnp.where(lane < 64, below, inner), jnp.where(lane < 64, inner, above)
        )
        mid = mix_x(oth[3, rows, :], nearest_post)
        inner = pick(own[3, rows, :], own_index)
        below, above = jnp.where(low, x_edge, mid), jnp.where(low, mid, x_edge)
        out[3, rows, :] = jnp.where(
            ix == 1, jnp.where(lane < 32, below, inner), jnp.where(lane >= 96, above, inner)
        )


def pad(base, ref, ghost, padded):
    _, iy, _ = positions(base)
    for t in range(TILES):
        rows = part(t)
        padded[0, 8 + 8 * t : 16 + 8 * t, :] = jnp.where(iy == 1, ghost[2, rows, :], 0.0)
        padded[SPAN + 1, 8 + 8 * t : 16 + 8 * t, :] = jnp.where(iy == 0, ghost[2, rows, :], 0.0)

    def layer(y, carry):
        for t in range(TILES):
            padded[y + 1, 8 + 8 * t : 16 + 8 * t, :] = ref[tile_row(y, t), :]
        padded[y + 1, 7:8, :] = ghost[0, pl.ds(y, 1), :]
        padded[y + 1, 40:41, :] = ghost[1, pl.ds(y, 1), :]
        return carry

    lax.fori_loop(0, SPAN, layer, 0, unroll=4)


def around(y, t, padded, ghost):
    lane = lanes()
    rows = slice(8 + 8 * t, 16 + 8 * t)
    own = padded[y + 1, rows, :]
    beyond = pick(ghost[3, part(t), :], 32 * (lane // 32) + y)
    return own, (
        jnp.where(lane % 32 == 0, beyond, turned(own, 1)),
        jnp.where(lane % 32 == 31, beyond, turned(own, 127)),
        padded[y, rows, :],
        padded[y + 2, rows, :],
        padded[y + 1, 7 + 8 * t : 15 + 8 * t, :],
        padded[y + 1, 9 + 8 * t : 17 + 8 * t, :],
    )


def parity(y):
    return (lax.broadcasted_iota(jnp.int32, (8, 128), 0) + lanes() + y) % 2


def inverted(x):
    guess = pl.reciprocal(x, approx=True)
    return guess * (2.0 - x * guess)


def collect_kernel(holder, v, f, k, c, kind, scalars, own, faces, bounds, hv, hf, hk, hc, hkind, sems):
    device = lax.axis_index(AXES)
    core = lax.rem(device, 2)
    source = (v, f, k, c, kind)
    landed = (hv, hf, hk, hc, hkind)
    copies = [pltpu.make_async_copy(source[i], landed[i], sems.at[i]) for i in range(5)]
    counting = pltpu.make_async_copy(holder, bounds, sems.at[5])
    order = (0, 2, 4, 1, 3)
    counting.start()
    for i in order:
        copies[i].start()
    counting.wait()
    count = []
    for bound in (0, 1, 2, 4, 6):
        count.append(jnp.sum((bounds[...] < device - core + bound).astype(jnp.int32)))
        scalars[len(count)] = count[-1]
    scalars[0] = core
    base = jnp.where(core == 0, count[0], count[1])
    for i in order:
        copies[i].wait()
        for j in range(8):
            block = landed[i][:, pl.ds(128 * j, 128)].T
            if i == 4:
                block = 1.0 - 0.5 * block.astype(F32)
            own[i, pl.ds(128 * j, 128), :] = block
        if i in (0, 2, 4):
            put_faces(base, own.at[i], faces.at[pl.ds(2 * i, 4)])


def window_of(scalars):
    core, extra = scalars[0], scalars[3] - scalars[1] - 4
    held = jnp.where(core == 0, scalars[2] - scalars[1], scalars[3] - scalars[2])
    lane = lanes()
    low = core == 0
    index = (lane + jnp.where(low, 0, 32 * held)) % 128
    index_other = (lane + jnp.where(low, 128 - 32 * held, 32 * extra)) % 128
    inside = (lane >= jnp.where(low, 0, 128 - 32 * held)) & (lane < jnp.where(low, 32 * held, 128))
    return lambda own, oth: jnp.where(inside, pick(own, index), pick(oth, index_other))


def face_window_kernel(scalars, own, oth, faces, sent):
    windowed = window_of(scalars)
    for i in range(12):
        for t in range(TILES):
            faces[i, part(t), :] = windowed(own[i, part(t), :], oth[i, part(t), :])
    put_sent(scalars, 1, faces, sent.at[0])
    for i in (1, 2):
        for t in range(TILES):
            z, nearest = outgoing(scalars, faces.at[pl.ds(4 * i, 4)], t, 0)
            sent[2 * i - 1, part(t), :] = z
            sent[2 * i, part(t), :] = nearest


def outgoing(scalars, faces, t, by):
    core = scalars[0]
    lane = (lanes() + 128 - by) % 128
    along_y = jnp.where(lane >= 64, 1, 0) == core
    y = faces[2, part(t), :]
    y = turned(y, by) if by else y
    x = pick(faces[3, part(t), :], (lane + 64 + 32 * core) % 128)
    return faces[core, part(t), :], jnp.where(along_y, y, x)


def put_sent(scalars, shade, faces, sent):
    mine = (lax.broadcasted_iota(jnp.int32, (8, 128), 0) + lanes() + scalars[0]) % 2 == shade
    for t in range(TILES):
        z, nearest = outgoing(scalars, faces, t, 1)
        sent[part(t), :] = jnp.where(mine, z, nearest)


def window_kernel(scalars, own, oth, window, inner):
    windowed = window_of(scalars)
    for i in range(5):

        def rows(y, carry):
            for t in range(TILES):
                at = tile_row(y, t)
                window[i, at, :] = windowed(own[i, at, :], oth[i, at, :])
            return carry

        lax.fori_loop(0, SPAN, rows, 0, unroll=8)

    row = lax.broadcasted_iota(jnp.int32, (8, 128), 0)

    def layer(y, carry):
        above = jnp.minimum(y + 1, SPAN - 1)
        heat = [window[2, tile_row(y, t), :] for t in range(TILES)]
        open_heat = [heat[t] * window[4, tile_row(y, t), :] for t in range(TILES)]
        heat_up = [pltpu.roll(x, 7, axis=0) for x in heat]
        open_up = [pltpu.roll(x, 7, axis=0) for x in open_heat]
        below = None
        for t in range(TILES):
            at = tile_row(y, t)
            doubled = 2.0 * open_heat[t]
            beside = doubled * turned(open_heat[t], 127) * inverted(heat[t] + turned(heat[t], 127))
            inner[0, at, :] = turned(beside, 1)
            inner[1, at, :] = beside
            heat2 = window[2, tile_row(above, t), :]
            inner[2, at, :] = doubled * window[4, tile_row(above, t), :] * heat2 * inverted(heat[t] + heat2)
            heat2, open2 = heat_up[t], open_up[t]
            if t < TILES - 1:
                heat2 = jnp.where(row == 7, heat_up[t + 1], heat2)
                open2 = jnp.where(row == 7, open_up[t + 1], open2)
            over = doubled * open2 * inverted(heat[t] + heat2)
            inner[4, at, :] = over
            lifted = pltpu.roll(over, 1, axis=0)
            inner[3, at, :] = lifted if below is None else jnp.where(row == 0, below, lifted)
            below = lifted
        return carry

    lax.fori_loop(0, SPAN, layer, 0, unroll=2)


def first_kernel(
    layers, scalars, fields, inner, own, oth, far, post, vo, fo, do, go, edge, faces, sent, ghost, pv, ends
):
    v, f, k, c, a = (fields.at[i] for i in range(5))
    where = whereabouts(scalars)
    base = where[1]
    ix, iy, iz = positions(base)
    lane = lanes()
    row = lax.broadcasted_iota(jnp.int32, (8, 128), 0)
    for number in range(3):
        group, outer = pl.ds(4 * number, 4), pl.ds(2 * number - 1, 2) if number else 0
        ghosts(where, own.at[group], oth.at[group], far.at[outer], post.at[outer], ghost.at[number])
    for t in range(TILES):
        rows = part(t)
        for face in range(4):
            heat, heat2 = own[4 + face, rows, :], ghost[1, face, rows, :]
            open_heat = heat * own[8 + face, rows, :]
            b = 2.0 * open_heat * ghost[2, face, rows, :] * heat2 * inverted(heat + heat2)
            edge[face, rows, :] = b
            if face < 2:
                ends[face, rows, :] = jnp.where(iz == (layers - 1 if face else 0), open_heat, b)
    pad(base, v, ghost.at[0], pv)
    low_in, low_out = (lane % 32 == 0) & (ix == 1), (lane % 32 == 0) & (ix == 0)
    high_in, high_out = (lane % 32 == 31) & (ix == 0), (lane % 32 == 31) & (ix == 1)

    def layer(y, carry):
        shade = parity(y)
        for t in range(TILES):
            rows = tile_row(y, t)
            value, values = around(y, t, pv, ghost.at[0])
            heat, opening = k[rows, :], a[rows, :]
            open_heat = heat * opening
            b_x = pick(edge[3, part(t), :], 32 * (lane // 32) + y)
            b_y = edge[2, part(t), :]
            b = [
                jnp.where(low_in, b_x, jnp.where(low_out, open_heat, inner[0, rows, :])),
                jnp.where(high_in, b_x, jnp.where(high_out, open_heat, inner[1, rows, :])),
                jnp.where(
                    y == 0, jnp.where(iy == 1, b_y, open_heat), inner[2, tile_row(jnp.maximum(y - 1, 0), t), :]
                ),
                jnp.where(y == SPAN - 1, jnp.where(iy == 0, b_y, open_heat), inner[2, rows, :]),
                inner[3, rows, :],
                inner[4, rows, :],
            ]
            if t == 0:
                b[4] = jnp.where(row == 0, ends[0, pl.ds(y, 1), :], b[4])
            if t == TILES - 1:
                b[5] = jnp.where(row == 7, ends[1, pl.ds(y, 1), :], b[5])
            summed = (b[0] + b[1]) + (b[2] + b[3]) + (b[4] + b[5])
            wall = jnp.where(opening == 0.5, heat, 0.0)
            diagonal = jnp.where(opening == 0.0, 1.0, c[rows, :] + summed + wall)
            inverse = inverted(diagonal)
            total = f[rows, :] * inverse
            fo[rows, :] = total
            do[rows, :] = diagonal
            b[0] = jnp.where(low_out, 0.0, b[0])
            b[1] = jnp.where(high_out, 0.0, b[1])
            for way in range(6):
                g = b[way] * inverse
                go[way, rows, :] = g
                total = total + g * values[way]
            vo[rows, :] = jnp.where(shade == 0, total, value)
        return carry

    lax.fori_loop(0, SPAN, layer, 0, unroll=4)
    put_faces(base, vo, faces)
    put_sent(scalars, 0, faces, sent)


def relaxed(y, t, f, g, padded, ghost):
    rows = tile_row(y, t)
    value, values = around(y, t, padded, ghost)
    total = f[rows, :]
    for way in range(6):
        total = total + g[way, rows, :] * values[way]
    return value, total


def sweep_kernel(shade_now, scalars, v, f, g, own, oth, far, post, vo, faces, *rest):
    *sent, ghost, padded = rest
    where = whereabouts(scalars)
    base = where[1]
    ghosts(where, own, oth, far, post, ghost)
    pad(base, v, ghost, padded)

    def layer(y, carry):
        shade = parity(y)
        for t in range(TILES):
            value, total = relaxed(y, t, f, g, padded, ghost)
            vo[tile_row(y, t), :] = jnp.where(shade == shade_now, total, value)
        return carry

    lax.fori_loop(0, SPAN, layer, 0, unroll=8)
    put_faces(base, vo, faces)
    if sent:
        put_sent(scalars, shade_now, faces, sent[0])


def residual_kernel(scalars, v, f, g, d, edge, own, oth, blocks, cross, ghost, padded, pair):
    where = whereabouts(scalars)
    core = where[0]
    ghosts(where, own, oth, None, None, ghost)
    pad(where[1], v, ghost, padded)
    lane = lanes()
    index = 2 * (lane % 64)

    def layer(y4, carry):
        for half in range(2):
            for t in range(TILES):
                added = None
                for step in range(2):
                    y = 4 * y4 + 2 * half + step
                    value, total = relaxed(y, t, f, g, padded, ghost)
                    rest = d[tile_row(y, t), :] * (total - value)
                    added = rest if added is None else added + rest
                pair[half, part(t), :] = added + turned(added, 127)
        for t in range(2):
            both = []
            for half in range(2):
                even = pair[half, pl.ds(16 * t, 8, stride=2), :]
                odd = pair[half, pl.ds(16 * t + 1, 8, stride=2), :]
                both.append(pick(even + odd, index))
            blocks[pl.ds(pl.multiple_of(16 * y4 + 8 * t, 8), 8), :] = (
                jnp.where(lane < 64, both[0], both[1]) * 0.125
            )
        return carry

    lax.fori_loop(0, 8, layer, 0, unroll=2)

    def pooled(face):
        for t in range(TILES):
            product = edge[face, part(t), :] * own[face, part(t), :]
            pair[0, part(t), :] = product + turned(product, 127)
        result = []
        for t in range(2):
            both = pair[0, pl.ds(16 * t, 8, stride=2), :] + pair[0, pl.ds(16 * t + 1, 8, stride=2), :]
            result.append(pick(both, index) * 0.125)
        return result

    for t, tile in enumerate(pooled(core)):
        cross[part(t), :] = tile
    for t, (along_y, along_x) in enumerate(zip(pooled(2), pooled(3))):
        cross[part(2 + t), :] = jnp.where(lane < 64, along_y, along_x)
    blocks[128:160, :] = cross[...]


def level_kernel(scalars, v, level, stack):
    core = scalars[0]
    held = jnp.where(core == 0, scalars[2] - scalars[1], scalars[3] - scalars[2])
    for j in range(8):
        stack[:, pl.ds(128 * j, 128)] = v[pl.ds(128 * j, 128), :].T
    for s in range(SLOTS):
        filled = s < held
        source = jnp.where(core == 0, s, jnp.where(filled, 4 - held + s, 0))
        for t in range(TILES):
            rows = pl.ds(pl.multiple_of(32 * source + 8 * t, 8), 8)
            level[s, part(t), :] = jnp.where(filled, stack[rows, :], 0.0)


def coarse_kernel(scalars, own, far, post, side, side_post, grid, table, crossing, joined):
    core = scalars[0]
    starts = [scalars[i] for i in (1, 3, 4, 5)]
    mine = jnp.where(core == 0, scalars[1], scalars[2])
    mine_end = jnp.where(core == 0, scalars[2], scalars[3])
    leader = lax.div(mine + 7, 8) * 8
    held = leader < mine_end
    low = core == 0
    lane = lanes()

    def child(patch):
        chip = (patch >= starts[1]).astype(jnp.int32) + (patch >= starts[2]).astype(jnp.int32)
        begin = jnp.where(chip == 0, starts[0], jnp.where(chip == 1, starts[1], starts[2]))
        end = jnp.where(chip == 0, starts[1], jnp.where(chip == 1, starts[2], starts[3]))
        return chip, patch - begin, end - begin

    def block(chip, j, count):
        entry = jnp.where(j < 4, j, j - count + 8)
        entry = jnp.clip(8 * chip + entry, 0, 19)
        return lax.div(entry, 4), lax.rem(entry, 4)

    @pl.when(held)
    def _():
        for t in range(16):
            rows = part(t)
            table[0, rows, :] = jnp.where(low, own[0, rows, :], own[1, rows, :])
            table[1, rows, :] = jnp.where(low, own[1, rows, :], own[0, rows, :])
            table[2, rows, :] = jnp.where(low, post[0, rows, :], far[0, rows, :])
            table[3, rows, :] = jnp.where(low, post[1, rows, :], far[1, rows, :])
            table[4, rows, :] = jnp.where(low, far[1, rows, :], post[1, rows, :])
        for t in range(4):
            rows, last = part(t), part(16 + t)
            crossing[0, rows, :] = jnp.where(low, side[rows, :], side_post[rows, :])
            crossing[1, rows, :] = jnp.where(low, own[1, last, :], own[0, last, :])
            crossing[2, rows, :] = jnp.where(low, post[1, last, :], far[1, last, :])
            crossing[3, rows, :] = jnp.where(low, post[0, last, :], far[0, last, :])
            crossing[4, rows, :] = jnp.where(low, far[1, last, :], post[1, last, :])
            crossing[5, rows, :] = jnp.where(low, side_post[rows, :], side[rows, :])

        def added(entry, rows, index, valid):
            tile = pick(crossing[jnp.clip(entry, 0, 5), rows, :], jnp.clip(index, 0, 127))
            return jnp.where(valid, tile, 0.0)

        for iy in range(2):
            for iz in range(2):
                left = child(leader + 2 * iy + 4 * iz)
                right = child(leader + 1 + 2 * iy + 4 * iz)
                left_block, left_slot = block(*left)
                right_block, right_slot = block(*right)
                for y in range(16):
                    for t in range(2):
                        rows = pl.ds(16 * (y // 2) + 8 * t, 8)
                        index = 64 * (y % 2) + lane % 16
                        a = pick(table[left_block, rows, :], index + 16 * left_slot)
                        b = pick(table[right_block, rows, :], index + 16 * right_slot)
                        joined[pl.ds(SPAN * (16 * iy + y) + 16 * iz + 8 * t, 8), :] = jnp.where(lane < 16, a, b)

                def pair_of(below, shift, rows):
                    tiles = []
                    for chip, j, count in (left, right):
                        place = j if below else j - count + 4 - shift
                        valid = (place < 4 - shift) if below else (place >= 0)
                        entry = chip if below else 3 + chip
                        slot = place + shift if below else place
                        tiles.append(added(entry, rows, 16 * slot + lane % 16, valid))
                    return jnp.where(lane < 16, tiles[0], tiles[1])

                first_row = SPAN * 16 * iy + 16 * iz
                for t in range(2):
                    at = pl.ds(first_row + 8 * SPAN * t, 8, stride=SPAN)
                    joined[at, :] = joined[at, :] + pair_of(True, 0, part(t))
                    at = pl.ds(first_row + 8 * SPAN * t + 15, 8, stride=SPAN)
                    joined[at, :] = joined[at, :] + pair_of(False, 0, part(t))
                    at = pl.ds(first_row + (0 if iy else 15 * SPAN) + 8 * t, 8)
                    joined[at, :] = joined[at, :] + pair_of(iy == 1, 2, part(2 + t))

                @pl.when(left[0] != right[0])
                def _():
                    for y in range(16):
                        for t in range(2):
                            at = pl.ds(first_row + SPAN * y + 8 * t, 8)
                            from_right = added(3 + left[0], part(2 + t), 0 * lane + 64 + y, True)
                            from_left = added(right[0], part(2 + t), 0 * lane + 112 + y, True)
                            side_tile = jnp.where(lane == 15, from_right, jnp.where(lane == 16, from_left, 0.0))
                            joined[at, :] = joined[at, :] + side_tile

        for j in range(8):
            turn = joined[pl.ds(128 * j, 128), :].T
            grid[0, :, pl.ds(128 * j, 128)] = turn[0:SPAN, :]

    @pl.when(jnp.logical_not(held))
    def _():
        grid[0] = jnp.zeros((SPAN, LAYER), F32)


def call(kernel, out_shape, operands, specs=None, out_specs=None, scratch=(), name=None, limit=32, leading=(SMEM,)):
    return pl.pallas_call(
        kernel,
        out_shape=out_shape,
        in_specs=list(leading) + (specs or [VMEM] * (len(operands) - 1)),
        out_specs=out_specs or jax.tree.map(lambda _: VMEM, out_shape),
        scratch_shapes=list(scratch),
        compiler_params=pltpu.CompilerParams(vmem_limit_bytes=limit * 1024 * 1024),
        name=name,
    )(*operands)


def shards(v, f, k, c, kind, holder):
    devices = lax.axis_size(AXES)
    swap = [(i, i ^ 1) for i in range(devices)]
    reach = [(i, i + 1) for i in range(1, devices - 1, 2)]
    reach = reach + [(b, a) for a, b in reach]
    patches = holder.shape[0]

    def exchange(faces, sent):
        far = lax.ppermute(sent, AXES, reach)
        oth = lax.ppermute(faces, AXES, swap)
        post = lax.ppermute(far, AXES, swap)
        return faces, oth, far, post

    fields = [x.reshape(SLOTS * SPAN, LAYER) for x in (v, f, k, c, kind)]
    five = jax.ShapeDtypeStruct((5, LAYER, 128), F32)
    twelve = jax.ShapeDtypeStruct((12, SPAN, 128), F32)
    sent_first = jax.ShapeDtypeStruct((5, SPAN, 128), F32)
    sent_later = jax.ShapeDtypeStruct((SPAN, 128), F32)
    scalars, own, faces = call(
        collect_kernel,
        [pltpu.SMEM((6,), jnp.int32), pltpu.VMEM(five.shape, F32), pltpu.VMEM(twelve.shape, F32)],
        [holder.reshape(patches // 128, 128), *fields],
        specs=[HBM] * 6,
        leading=[],
        out_specs=[SMEM, VMEM, VMEM],
        scratch=[pltpu.VMEM((patches // 128, 128), jnp.int32)]
        + [pltpu.VMEM(x.shape, x.dtype) for x in fields]
        + [pltpu.SemaphoreType.DMA((6,))],
        name="collect",
        limit=COLLECT_LIMIT,
    )
    faces, sent = call(
        face_window_kernel,
        [twelve, sent_first],
        [scalars, faces, lax.ppermute(faces, AXES, swap)],
        name="face_window",
    )
    sent, own = lax.optimization_barrier((sent, own))
    far = lax.ppermute(sent, AXES, reach)
    oth = lax.ppermute(faces, AXES, swap)
    window, inner = call(window_kernel, [five, five], [scalars, own, lax.ppermute(own, AXES, swap)], name="window")
    far, window, inner = lax.optimization_barrier((far, window, inner))
    post = lax.ppermute(far, AXES, swap)
    coefficients = jax.ShapeDtypeStruct((6, LAYER, 128), F32)
    wv, wf, wd, wg, edge, faces, *sent = call(
        functools.partial(first_kernel, patches // 4),
        [FIELD, FIELD, FIELD, coefficients, FACES, FACES, sent_later],
        [scalars, window, inner, faces, oth, far, post],
        scratch=[pltpu.VMEM((3, 4, SPAN, 128), F32), PADDED, pltpu.VMEM((2, SPAN, 128), F32)],
        name="first",
    )
    for shade, more in ((1, [sent_later]), (0, [sent_later]), (1, [])):
        wv, faces, *sent = call(
            functools.partial(sweep_kernel, shade),
            [FIELD, FACES] + more,
            [scalars, wv, wf, wg, *exchange(faces, *sent)],
            scratch=[GHOSTS, PADDED],
            name="sweep",
        )
    blocks, cross = call(
        residual_kernel,
        [jax.ShapeDtypeStruct((160, 128), F32), jax.ShapeDtypeStruct((SPAN, 128), F32)],
        [scalars, wv, wf, wg, wd, edge, faces, lax.ppermute(faces, AXES, swap)],
        scratch=[GHOSTS, PADDED, pltpu.VMEM((2, SPAN, 128), F32)],
        name="residual",
    )
    beside = [(i, i - 5) for i in range(6, devices, 2)] + [(i, i + 1) for i in range(1, devices - 1, 2)]
    both = jnp.stack([blocks, lax.ppermute(blocks, AXES, swap)], 0)
    downward = [(i, i - 1) for i in range(2, devices, 2)] + [(i, i - 5) for i in range(5, devices, 2)]
    far = lax.ppermute(both, AXES, downward)
    side = lax.ppermute(cross, AXES, beside)
    level = call(
        level_kernel,
        jax.ShapeDtypeStruct((SLOTS, SPAN, LAYER), F32),
        [scalars, wv],
        scratch=[pltpu.VMEM((128, LAYER), F32)],
        name="level",
    )
    side, far, level = lax.optimization_barrier((side, far, level))
    post = lax.ppermute(far, AXES, swap)
    side_post = lax.ppermute(side, AXES, swap)
    grid = call(
        coarse_kernel,
        jax.ShapeDtypeStruct((1, SPAN, LAYER), F32),
        [scalars, both, far, post, side, side_post],
        scratch=[pltpu.VMEM((5, 128, 128), F32), pltpu.VMEM((6, SPAN, 128), F32), pltpu.VMEM((LAYER, 128), F32)],
        name="coarse",
    )
    return level, grid


def solution(mesh):
    spec = P(AXES, None, None)
    return jax.shard_map(
        shards,
        mesh=mesh,
        in_specs=(spec, spec, spec, spec, spec, P()),
        out_specs=(spec, spec),
        check_vma=False,
    )
```

```python
import functools

import jax
import jax.numpy as jnp
from jax import lax
from jax.experimental import pallas as pl
from jax.experimental.pallas import tpu as pltpu
from jax.sharding import PartitionSpec as P

COLLECT_LIMIT = 56
AXES = ("wide", "narrow")
SPAN = 32
LAYER = 1024
SLOTS = 4
TILES = 4
F32 = jnp.float32
VMEM = pl.BlockSpec(memory_space=pltpu.VMEM)
SMEM = pl.BlockSpec(memory_space=pltpu.SMEM)
HBM = pl.BlockSpec(memory_space=pl.ANY)
FACES = jax.ShapeDtypeStruct((4, SPAN, 128), F32)
FIELD = jax.ShapeDtypeStruct((LAYER, 128), F32)
GHOSTS = pltpu.VMEM((4, SPAN, 128), F32)
PADDED = pltpu.VMEM((SPAN + 2, 48, 128), F32)


def lanes():
    return lax.broadcasted_iota(jnp.int32, (8, 128), 1)


def pick(tile, index):
    return jnp.take_along_axis(tile, index, axis=1, mode="promise_in_bounds")


def turned(tile, by):
    return pltpu.roll(tile, by, axis=1)


def part(xt):
    return pl.ds(8 * xt, 8)


def tile_row(y, zt):
    return pl.ds(pl.multiple_of(SPAN * y + 8 * zt, 8), 8)


def whereabouts(scalars):
    core = scalars[0]
    first, last = scalars[1], scalars[3]
    return core, jnp.where(core == 0, first, last - 4), last - first - 4


def positions(base):
    patch = base + lanes() // 32
    return patch % 2, (patch // 2) % 2, patch // 4


def put_faces(base, ref, faces):
    ix, iy, _ = positions(base)
    lane = lanes()
    for t in range(TILES):
        faces[0, part(t), :] = ref[pl.ds(256 * t, 8, stride=SPAN), :]
        faces[1, part(t), :] = ref[pl.ds(256 * t + 31, 8, stride=SPAN), :]
        faces[2, part(t), :] = jnp.where(iy == 1, ref[part(t), :], ref[pl.ds(31 * SPAN + 8 * t, 8), :])
    index = 32 * (lane // 32) + jnp.where(ix == 1, 0, 31)
    for t in range(TILES):
        found = pick(ref[part(t), :], index)
        for y in range(1, SPAN):
            found = jnp.where(lane % 32 == y, pick(ref[pl.ds(SPAN * y + 8 * t, 8), :], index), found)
        faces[3, part(t), :] = found


def ghosts(where, own, oth, far, post, out):
    core, base, extra = where
    lane = lanes()
    ix, iy, _ = positions(base)
    low = core == 0
    start = jnp.where(low, 4 - extra, extra)
    single = 1 if far is not None and len(far.shape) == 2 else 0
    x_far = jnp.where(low, 32, 64) + single
    x_post = jnp.where(low, 64, 32) + single
    x_turn = jnp.where(low, 96, 32)

    def mixer(turn, lift):
        target = (lane + turn) % 128
        index, index_post = (target + 32 * start) % 128, (target + 32 * start + lift) % 128
        here = jnp.where(target < 128 - 32 * start, 1, 0) == 1 - core
        if oth is None:
            return lambda a, b: jnp.zeros((8, 128), F32)
        return lambda a, b: jnp.where(here, pick(a, index), pick(b, index_post))

    mix_z, mix_y, mix_x = mixer(0, 0), mixer(64, single), mixer(128 - x_turn, x_post)
    y_index = (lane + 64 + single) % 128
    x_index = (lane + x_far + jnp.where(low, 96, 32)) % 128
    own_index = jnp.where(ix == 1, lane + 96, lane + 32) % 128
    for t in range(TILES):
        rows = part(t)
        if far is None:
            z_edge = y_edge = x_edge = 0.0
            z_post = nearest_post = None
        else:
            z_edge = far[rows, :] if single else far[0, rows, :]
            nearest = z_edge if single else far[1, rows, :]
            z_post = post[rows, :] if single else post[0, rows, :]
            nearest_post = z_post if single else post[1, rows, :]
            y_edge, x_edge = pick(nearest, y_index), pick(nearest, x_index)
        others = (None,) * 3 if oth is None else (oth[core, rows, :], oth[2, rows, :], oth[3, rows, :])
        mid = mix_z(others[0], z_post)
        out[0, rows, :], out[1, rows, :] = jnp.where(low, z_edge, mid), jnp.where(low, mid, z_edge)
        mid = mix_y(others[1], nearest_post)
        inner = turned(own[2, rows, :], 64)
        below, above = jnp.where(low, y_edge, mid), jnp.where(low, mid, y_edge)
        out[2, rows, :] = jnp.where(
            iy == 1, jnp.where(lane < 64, below, inner), jnp.where(lane < 64, inner, above)
        )
        mid = mix_x(others[2], nearest_post)
        inner = pick(own[3, rows, :], own_index)
        below, above = jnp.where(low, x_edge, mid), jnp.where(low, mid, x_edge)
        out[3, rows, :] = jnp.where(
            ix == 1, jnp.where(lane < 32, below, inner), jnp.where(lane >= 96, above, inner)
        )


def pad(base, ref, ghost, padded):
    _, iy, _ = positions(base)
    for t in range(TILES):
        rows = part(t)
        padded[0, 8 + 8 * t : 16 + 8 * t, :] = jnp.where(iy == 1, ghost[2, rows, :], 0.0)
        padded[SPAN + 1, 8 + 8 * t : 16 + 8 * t, :] = jnp.where(iy == 0, ghost[2, rows, :], 0.0)

    def layer(y, carry):
        for t in range(TILES):
            padded[y + 1, 8 + 8 * t : 16 + 8 * t, :] = ref[tile_row(y, t), :]
        padded[y + 1, 7:8, :] = ghost[0, pl.ds(y, 1), :]
        padded[y + 1, 40:41, :] = ghost[1, pl.ds(y, 1), :]
        return carry

    lax.fori_loop(0, SPAN, layer, 0, unroll=4)


def around(y, t, padded, ghost):
    lane = lanes()
    rows = slice(8 + 8 * t, 16 + 8 * t)
    own = padded[y + 1, rows, :]
    beyond = pick(ghost[3, part(t), :], 32 * (lane // 32) + y)
    return own, (
        jnp.where(lane % 32 == 0, beyond, turned(own, 1)),
        jnp.where(lane % 32 == 31, beyond, turned(own, 127)),
        padded[y, rows, :],
        padded[y + 2, rows, :],
        padded[y + 1, 7 + 8 * t : 15 + 8 * t, :],
        padded[y + 1, 9 + 8 * t : 17 + 8 * t, :],
    )


def parity(y):
    return (lax.broadcasted_iota(jnp.int32, (8, 128), 0) + lanes() + y) % 2


def inverted(x):
    guess = pl.reciprocal(x, approx=True)
    return guess * (2.0 - x * guess)


def collect_kernel(holder, v, k, kind, scalars, own, faces, bounds, hv, hk, hkind, sems):
    device = lax.axis_index(AXES)
    core = lax.rem(device, 2)
    landed = (hv, hk, hkind)
    copies = [pltpu.make_async_copy(ref, landed[i], sems.at[i]) for i, ref in enumerate((v, k, kind))]
    counting = pltpu.make_async_copy(holder, bounds, sems.at[3])
    counting.start()
    for copy in copies:
        copy.start()
    counting.wait()
    count = []
    for bound in (0, 1, 2, 4, 6):
        count.append(jnp.sum((bounds[...] < device - core + bound).astype(jnp.int32)))
        scalars[len(count)] = count[-1]
    scalars[0] = core
    base = jnp.where(core == 0, count[0], count[1])
    for i in range(3):
        copies[i].wait()
        for j in range(8):
            block = landed[i][:, pl.ds(128 * j, 128)].T
            if i == 2:
                block = 1.0 - 0.5 * block.astype(F32)
            own[i, pl.ds(128 * j, 128), :] = block
        put_faces(base, own.at[i], faces.at[pl.ds(4 * i, 4)])


def collect_rest_kernel(f, c, own, hf, hc, sems):
    landed = (hf, hc)
    copies = [pltpu.make_async_copy(ref, landed[i], sems.at[i]) for i, ref in enumerate((f, c))]
    for copy in copies:
        copy.start()
    for i in range(2):
        copies[i].wait()
        for j in range(8):
            own[i, pl.ds(128 * j, 128), :] = landed[i][:, pl.ds(128 * j, 128)].T


def window_of(scalars):
    core, extra = scalars[0], scalars[3] - scalars[1] - 4
    held = jnp.where(core == 0, scalars[2] - scalars[1], scalars[3] - scalars[2])
    lane = lanes()
    low = core == 0
    index = (lane + jnp.where(low, 0, 32 * held)) % 128
    index_other = (lane + jnp.where(low, 128 - 32 * held, 32 * extra)) % 128
    inside = (lane >= jnp.where(low, 0, 128 - 32 * held)) & (lane < jnp.where(low, 32 * held, 128))
    return lambda own, oth: jnp.where(inside, pick(own, index), pick(oth, index_other))


def face_window_kernel(scalars, own, oth, faces, sent):
    windowed = window_of(scalars)
    for i in range(12):
        for t in range(TILES):
            faces[i, part(t), :] = windowed(own[i, part(t), :], oth[i, part(t), :])
    put_sent(scalars, 1, faces, sent.at[0])
    for i in (1, 2):
        for t in range(TILES):
            z, nearest = outgoing(scalars, faces.at[pl.ds(4 * i, 4)], t, 0)
            sent[2 * i - 1, part(t), :] = z
            sent[2 * i, part(t), :] = nearest


def outgoing(scalars, faces, t, by):
    core = scalars[0]
    lane = (lanes() + 128 - by) % 128
    along_y = jnp.where(lane >= 64, 1, 0) == core
    y = faces[2, part(t), :]
    y = turned(y, by) if by else y
    x = pick(faces[3, part(t), :], (lane + 64 + 32 * core) % 128)
    return faces[core, part(t), :], jnp.where(along_y, y, x)


def put_sent(scalars, shade, faces, sent):
    mine = (lax.broadcasted_iota(jnp.int32, (8, 128), 0) + lanes() + scalars[0]) % 2 == shade
    for t in range(TILES):
        z, nearest = outgoing(scalars, faces, t, 1)
        sent[part(t), :] = jnp.where(mine, z, nearest)


def window_kernel(scalars, own, oth, own_rest, oth_rest, window, inner):
    windowed = window_of(scalars)
    for i in range(5):
        mine, theirs = (own.at[i], oth.at[i]) if i < 3 else (own_rest.at[i - 3], oth_rest.at[i - 3])

        def rows(y, carry):
            for t in range(TILES):
                at = tile_row(y, t)
                window[i, at, :] = windowed(mine[at, :], theirs[at, :])
            return carry

        lax.fori_loop(0, SPAN, rows, 0, unroll=8)

    row = lax.broadcasted_iota(jnp.int32, (8, 128), 0)

    def layer(y, carry):
        above = jnp.minimum(y + 1, SPAN - 1)
        heat = [window[1, tile_row(y, t), :] for t in range(TILES)]
        open_heat = [heat[t] * window[2, tile_row(y, t), :] for t in range(TILES)]
        heat_up = [pltpu.roll(x, 7, axis=0) for x in heat]
        open_up = [pltpu.roll(x, 7, axis=0) for x in open_heat]
        below = None
        for t in range(TILES):
            at = tile_row(y, t)
            doubled = 2.0 * open_heat[t]
            beside = doubled * turned(open_heat[t], 127) * inverted(heat[t] + turned(heat[t], 127))
            inner[0, at, :] = turned(beside, 1)
            inner[1, at, :] = beside
            heat2 = window[1, tile_row(above, t), :]
            inner[2, at, :] = doubled * window[2, tile_row(above, t), :] * heat2 * inverted(heat[t] + heat2)
            heat2, open2 = heat_up[t], open_up[t]
            if t < TILES - 1:
                heat2 = jnp.where(row == 7, heat_up[t + 1], heat2)
                open2 = jnp.where(row == 7, open_up[t + 1], open2)
            over = doubled * open2 * inverted(heat[t] + heat2)
            inner[4, at, :] = over
            lifted = pltpu.roll(over, 1, axis=0)
            inner[3, at, :] = lifted if below is None else jnp.where(row == 0, below, lifted)
            below = lifted
        return carry

    lax.fori_loop(0, SPAN, layer, 0, unroll=4)


def first_kernel(
    layers, scalars, fields, inner, own, oth, far, post, vo, fo, do, go, edge, faces, sent, ghost, pv, ends
):
    v, k, a, f, c = (fields.at[i] for i in range(5))
    where = whereabouts(scalars)
    base = where[1]
    ix, iy, iz = positions(base)
    lane = lanes()
    row = lax.broadcasted_iota(jnp.int32, (8, 128), 0)
    for number in range(3):
        group, outer = pl.ds(4 * number, 4), pl.ds(2 * number - 1, 2) if number else 0
        ghosts(where, own.at[group], oth.at[group], far.at[outer], post.at[outer], ghost.at[number])
    for t in range(TILES):
        rows = part(t)
        for face in range(4):
            heat, heat2 = own[4 + face, rows, :], ghost[1, face, rows, :]
            open_heat = heat * own[8 + face, rows, :]
            b = 2.0 * open_heat * ghost[2, face, rows, :] * heat2 * inverted(heat + heat2)
            edge[face, rows, :] = b
            if face < 2:
                ends[face, rows, :] = jnp.where(iz == (layers - 1 if face else 0), open_heat, b)
    pad(base, v, ghost.at[0], pv)
    low_in, low_out = (lane % 32 == 0) & (ix == 1), (lane % 32 == 0) & (ix == 0)
    high_in, high_out = (lane % 32 == 31) & (ix == 0), (lane % 32 == 31) & (ix == 1)

    def layer(y, carry):
        shade = parity(y)
        for t in range(TILES):
            rows = tile_row(y, t)
            value, values = around(y, t, pv, ghost.at[0])
            heat, opening = k[rows, :], a[rows, :]
            open_heat = heat * opening
            b_x = pick(edge[3, part(t), :], 32 * (lane // 32) + y)
            b_y = edge[2, part(t), :]
            b = [
                jnp.where(low_in, b_x, jnp.where(low_out, open_heat, inner[0, rows, :])),
                jnp.where(high_in, b_x, jnp.where(high_out, open_heat, inner[1, rows, :])),
                jnp.where(
                    y == 0, jnp.where(iy == 1, b_y, open_heat), inner[2, tile_row(jnp.maximum(y - 1, 0), t), :]
                ),
                jnp.where(y == SPAN - 1, jnp.where(iy == 0, b_y, open_heat), inner[2, rows, :]),
                inner[3, rows, :],
                inner[4, rows, :],
            ]
            if t == 0:
                b[4] = jnp.where(row == 0, ends[0, pl.ds(y, 1), :], b[4])
            if t == TILES - 1:
                b[5] = jnp.where(row == 7, ends[1, pl.ds(y, 1), :], b[5])
            summed = (b[0] + b[1]) + (b[2] + b[3]) + (b[4] + b[5])
            wall = jnp.where(opening == 0.5, heat, 0.0)
            diagonal = jnp.where(opening == 0.0, 1.0, c[rows, :] + summed + wall)
            inverse = inverted(diagonal)
            total = f[rows, :] * inverse
            fo[rows, :] = total
            do[rows, :] = diagonal
            b[0] = jnp.where(low_out, 0.0, b[0])
            b[1] = jnp.where(high_out, 0.0, b[1])
            for way in range(6):
                g = b[way] * inverse
                go[way, rows, :] = g
                total = total + g * values[way]
            vo[rows, :] = jnp.where(shade == 0, total, value)
        return carry

    lax.fori_loop(0, SPAN, layer, 0, unroll=4)
    put_faces(base, vo, faces)
    put_sent(scalars, 0, faces, sent)


def relaxed(y, t, f, g, padded, ghost):
    rows = tile_row(y, t)
    value, values = around(y, t, padded, ghost)
    total = f[rows, :]
    for way in range(6):
        total = total + g[way, rows, :] * values[way]
    return value, total


def sweep_kernel(shade_now, scalars, v, f, g, own, oth, far, post, vo, faces, *rest):
    *sent, ghost, padded = rest
    where = whereabouts(scalars)
    base = where[1]
    ghosts(where, own, oth, far, post, ghost)
    pad(base, v, ghost, padded)

    def layer(y, carry):
        shade = parity(y)
        for t in range(TILES):
            value, total = relaxed(y, t, f, g, padded, ghost)
            vo[tile_row(y, t), :] = jnp.where(shade == shade_now, total, value)
        return carry

    lax.fori_loop(0, SPAN, layer, 0, unroll=8)
    put_faces(base, vo, faces)
    if sent:
        put_sent(scalars, shade_now, faces, sent[0])


def residual_kernel(scalars, v, f, g, d, edge, own, blocks, cross, ghost, padded, pair):
    where = whereabouts(scalars)
    core = where[0]
    ghosts(where, own, None, None, None, ghost)
    pad(where[1], v, ghost, padded)
    lane = lanes()
    index = 2 * (lane % 64)

    def layer(y4, carry):
        for half in range(2):
            for t in range(TILES):
                added = None
                for step in range(2):
                    y = 4 * y4 + 2 * half + step
                    value, total = relaxed(y, t, f, g, padded, ghost)
                    rest = d[tile_row(y, t), :] * (total - value)
                    added = rest if added is None else added + rest
                pair[half, part(t), :] = added + turned(added, 127)
        for t in range(2):
            both = []
            for half in range(2):
                even = pair[half, pl.ds(16 * t, 8, stride=2), :]
                odd = pair[half, pl.ds(16 * t + 1, 8, stride=2), :]
                both.append(pick(even + odd, index))
            blocks[pl.ds(pl.multiple_of(16 * y4 + 8 * t, 8), 8), :] = (
                jnp.where(lane < 64, both[0], both[1]) * 0.125
            )
        return carry

    lax.fori_loop(0, 8, layer, 0, unroll=2)

    def pooled(face):
        for t in range(TILES):
            product = edge[face, part(t), :] * own[face, part(t), :]
            pair[0, part(t), :] = product + turned(product, 127)
        result = []
        for t in range(2):
            both = pair[0, pl.ds(16 * t, 8, stride=2), :] + pair[0, pl.ds(16 * t + 1, 8, stride=2), :]
            result.append(pick(both, index) * 0.125)
        return result

    for t, (z_low, z_high, along_y, along_x) in enumerate(zip(*(pooled(face) for face in range(4)))):
        blocks[128 + 8 * t : 136 + 8 * t, :] = z_low
        blocks[144 + 8 * t : 152 + 8 * t, :] = z_high
        blocks[160 + 8 * t : 168 + 8 * t, :] = jnp.where(lane < 64, along_y, along_x)
        cross[part(t), :] = jnp.where(core == 0, z_low, z_high)


def level_kernel(scalars, v, level, stack):
    core = scalars[0]
    held = jnp.where(core == 0, scalars[2] - scalars[1], scalars[3] - scalars[2])
    for j in range(8):
        stack[:, pl.ds(128 * j, 128)] = v[pl.ds(128 * j, 128), :].T
    for s in range(SLOTS):
        filled = s < held
        source = jnp.where(core == 0, s, jnp.where(filled, 4 - held + s, 0))
        for t in range(TILES):
            rows = pl.ds(pl.multiple_of(32 * source + 8 * t, 8), 8)
            level[s, part(t), :] = jnp.where(filled, stack[rows, :], 0.0)


def coarse_kernel(scalars, own, far, post, side, side_post, grid, table, crossing, joined):
    core = scalars[0]
    starts = [scalars[i] for i in (1, 3, 4, 5)]
    mine = jnp.where(core == 0, scalars[1], scalars[2])
    mine_end = jnp.where(core == 0, scalars[2], scalars[3])
    leader = lax.div(mine + 7, 8) * 8
    held = leader < mine_end
    low = core == 0
    lane = lanes()

    def child(patch):
        chip = (patch >= starts[1]).astype(jnp.int32) + (patch >= starts[2]).astype(jnp.int32)
        begin = jnp.where(chip == 0, starts[0], jnp.where(chip == 1, starts[1], starts[2]))
        end = jnp.where(chip == 0, starts[1], jnp.where(chip == 1, starts[2], starts[3]))
        return chip, patch - begin, end - begin

    def block(chip, j, count):
        entry = jnp.where(j < 4, j, j - count + 8)
        entry = jnp.clip(8 * chip + entry, 0, 19)
        return lax.div(entry, 4), lax.rem(entry, 4)

    @pl.when(held)
    def _():
        for t in range(16):
            rows = part(t)
            table[0, rows, :] = jnp.where(low, own[0, rows, :], own[1, rows, :])
            table[1, rows, :] = jnp.where(low, own[1, rows, :], own[0, rows, :])
            table[2, rows, :] = jnp.where(low, post[0, rows, :], far[0, rows, :])
            table[3, rows, :] = jnp.where(low, post[1, rows, :], far[1, rows, :])
            table[4, rows, :] = jnp.where(low, far[1, rows, :], post[1, rows, :])
        for t in range(6):
            rows, last = part(t), part(16 + t)
            crossing[2, rows, :] = jnp.where(low, own[0, last, :], own[1, last, :])
            crossing[3, rows, :] = jnp.where(low, own[1, last, :], own[0, last, :])
            crossing[4, rows, :] = jnp.where(low, post[0, last, :], far[0, last, :])
            crossing[5, rows, :] = jnp.where(low, post[1, last, :], far[1, last, :])
            crossing[6, rows, :] = jnp.where(low, far[1, last, :], post[1, last, :])
            crossing[7, rows, :] = jnp.where(low, far[0, last, :], post[0, last, :])
        for t in range(2):
            rows = part(t)
            crossing[1, part(2 + t), :] = jnp.where(low, side[rows, :], side_post[rows, :])
            crossing[8, rows, :] = jnp.where(low, side_post[rows, :], side[rows, :])

        def giver(chip, j, count, step):
            q = j + step
            in_first = j < 4
            begin = jnp.where(in_first, 0, count - 4)
            valid = (q < begin) | (q >= begin + 4)
            entry = 2 * chip + jnp.where(q < 0, 1, jnp.where(q >= count, 4, jnp.where(in_first, 3, 2)))
            slot = jnp.where(
                q < 0, q + 4, jnp.where(q >= count, q - count, jnp.where(in_first, q - count + 4, q))
            )
            return valid, jnp.clip(entry, 1, 8), slot

        def added(source, rows, index):
            valid, entry, slot = source
            return jnp.where(valid, pick(crossing[entry, rows, :], (index + 16 * slot) % 128), 0.0)

        for iy in range(2):
            for iz in range(2):
                left = child(leader + 2 * iy + 4 * iz)
                right = child(leader + 1 + 2 * iy + 4 * iz)
                left_block, left_slot = block(*left)
                right_block, right_slot = block(*right)
                for y in range(16):
                    for t in range(2):
                        rows = pl.ds(16 * (y // 2) + 8 * t, 8)
                        index = 64 * (y % 2) + lane % 16
                        a = pick(table[left_block, rows, :], index + 16 * left_slot)
                        b = pick(table[right_block, rows, :], index + 16 * right_slot)
                        joined[pl.ds(SPAN * (16 * iy + y) + 16 * iz + 8 * t, 8), :] = jnp.where(lane < 16, a, b)

                def pair_of(step, rows):
                    tiles = [added(giver(*one, step), rows, lane % 16) for one in (left, right)]
                    return jnp.where(lane < 16, tiles[0], tiles[1])

                first_row = SPAN * 16 * iy + 16 * iz
                for t in range(2):
                    at = pl.ds(first_row + 8 * SPAN * t, 8, stride=SPAN)
                    joined[at, :] = joined[at, :] + pair_of(-4, part(2 + t))
                    at = pl.ds(first_row + 8 * SPAN * t + 15, 8, stride=SPAN)
                    joined[at, :] = joined[at, :] + pair_of(4, part(t))
                    at = pl.ds(first_row + (0 if iy else 15 * SPAN) + 8 * t, 8)
                    joined[at, :] = joined[at, :] + pair_of(-2 if iy else 2, part(4 + t))
                from_right, from_left = giver(*left, 1), giver(*right, -1)

                @pl.when(from_right[0] | from_left[0])
                def _():
                    for y in range(16):
                        for t in range(2):
                            at = pl.ds(first_row + SPAN * y + 8 * t, 8)
                            high = added(from_right, part(4 + t), 0 * lane + 64 + y)
                            low_side = added(from_left, part(4 + t), 0 * lane + 64 + y)
                            side_tile = jnp.where(lane == 15, high, jnp.where(lane == 16, low_side, 0.0))
                            joined[at, :] = joined[at, :] + side_tile

        for j in range(8):
            turn = joined[pl.ds(128 * j, 128), :].T
            grid[0, :, pl.ds(128 * j, 128)] = turn[0:SPAN, :]

    @pl.when(jnp.logical_not(held))
    def _():
        grid[0] = jnp.zeros((SPAN, LAYER), F32)


def call(kernel, out_shape, operands, specs=None, out_specs=None, scratch=(), name=None, limit=32, leading=(SMEM,)):
    return pl.pallas_call(
        kernel,
        out_shape=out_shape,
        in_specs=list(leading) + (specs or [VMEM] * (len(operands) - 1)),
        out_specs=out_specs or jax.tree.map(lambda _: VMEM, out_shape),
        scratch_shapes=list(scratch),
        compiler_params=pltpu.CompilerParams(vmem_limit_bytes=limit * 1024 * 1024),
        name=name,
    )(*operands)


def shards(v, f, k, c, kind, holder):
    devices = lax.axis_size(AXES)
    swap = [(i, i ^ 1) for i in range(devices)]
    reach = [(i, i + 1) for i in range(1, devices - 1, 2)]
    reach = reach + [(b, a) for a, b in reach]
    patches = holder.shape[0]

    def exchange(faces, sent):
        far = lax.ppermute(sent, AXES, reach)
        oth = lax.ppermute(faces, AXES, swap)
        post = lax.ppermute(far, AXES, swap)
        return faces, oth, far, post

    v, f, k, c, kind = (x.reshape(SLOTS * SPAN, LAYER) for x in (v, f, k, c, kind))
    five = jax.ShapeDtypeStruct((5, LAYER, 128), F32)
    twelve = jax.ShapeDtypeStruct((12, SPAN, 128), F32)
    sent_first = jax.ShapeDtypeStruct((5, SPAN, 128), F32)
    sent_later = jax.ShapeDtypeStruct((SPAN, 128), F32)
    landing = pltpu.VMEM((SLOTS * SPAN, LAYER), F32)
    scalars, own, faces = call(
        collect_kernel,
        [pltpu.SMEM((6,), jnp.int32), pltpu.VMEM((3, LAYER, 128), F32), pltpu.VMEM(twelve.shape, F32)],
        [holder.reshape(patches // 128, 128), v, k, kind],
        specs=[HBM] * 4,
        leading=[],
        out_specs=[SMEM, VMEM, VMEM],
        scratch=[pltpu.VMEM((patches // 128, 128), jnp.int32), landing, landing]
        + [pltpu.VMEM((SLOTS * SPAN, LAYER), jnp.int32), pltpu.SemaphoreType.DMA((4,))],
        name="collect",
        limit=COLLECT_LIMIT,
    )
    own_rest = call(
        collect_rest_kernel,
        pltpu.VMEM((2, LAYER, 128), F32),
        [f, c],
        specs=[HBM] * 2,
        leading=[],
        out_specs=VMEM,
        scratch=[landing, landing, pltpu.SemaphoreType.DMA((2,))],
        name="collect_rest",
        limit=COLLECT_LIMIT,
    )
    oth, own_rest = lax.optimization_barrier((lax.ppermute(faces, AXES, swap), own_rest))
    faces, sent = call(
        face_window_kernel,
        [twelve, sent_first],
        [scalars, faces, oth],
        name="face_window",
    )
    sent, own, own_rest = lax.optimization_barrier((sent, own, own_rest))
    far = lax.ppermute(sent, AXES, reach)
    oth = lax.ppermute(faces, AXES, swap)
    window, inner = call(
        window_kernel,
        [five, five],
        [scalars, own, lax.ppermute(own, AXES, swap), own_rest, lax.ppermute(own_rest, AXES, swap)],
        name="window",
    )
    far, window, inner = lax.optimization_barrier((far, window, inner))
    post = lax.ppermute(far, AXES, swap)
    coefficients = jax.ShapeDtypeStruct((6, LAYER, 128), F32)
    wv, wf, wd, wg, edge, faces, *sent = call(
        functools.partial(first_kernel, patches // 4),
        [FIELD, FIELD, FIELD, coefficients, FACES, FACES, sent_later],
        [scalars, window, inner, faces, oth, far, post],
        scratch=[pltpu.VMEM((3, 4, SPAN, 128), F32), PADDED, pltpu.VMEM((2, SPAN, 128), F32)],
        name="first",
    )
    for shade, more in ((1, [sent_later]), (0, [sent_later]), (1, [])):
        wv, faces, *sent = call(
            functools.partial(sweep_kernel, shade),
            [FIELD, FACES] + more,
            [scalars, wv, wf, wg, *exchange(faces, *sent)],
            scratch=[GHOSTS, PADDED],
            name="sweep",
        )
    blocks, cross = call(
        residual_kernel,
        [jax.ShapeDtypeStruct((176, 128), F32), jax.ShapeDtypeStruct((16, 128), F32)],
        [scalars, wv, wf, wg, wd, edge, faces],
        scratch=[GHOSTS, PADDED, pltpu.VMEM((2, SPAN, 128), F32)],
        name="residual",
    )
    beside = [(i, i - 5) for i in range(6, devices, 2)] + [(i, i + 1) for i in range(1, devices - 1, 2)]
    both = jnp.stack([blocks, lax.ppermute(blocks, AXES, swap)], 0)
    downward = [(i, i - 1) for i in range(2, devices, 2)] + [(i, i - 5) for i in range(5, devices, 2)]
    far = lax.ppermute(both, AXES, downward)
    side = lax.ppermute(cross, AXES, beside)
    far, wv = lax.optimization_barrier((far, wv))
    level = call(
        level_kernel,
        jax.ShapeDtypeStruct((SLOTS, SPAN, LAYER), F32),
        [scalars, wv],
        scratch=[pltpu.VMEM((128, LAYER), F32)],
        name="level",
    )
    side, level = lax.optimization_barrier((side, level))
    side, far = lax.optimization_barrier((side, far))
    post = lax.ppermute(far, AXES, swap)
    side_post = lax.ppermute(side, AXES, swap)
    grid = call(
        coarse_kernel,
        jax.ShapeDtypeStruct((1, SPAN, LAYER), F32),
        [scalars, both, far, post, side, side_post],
        scratch=[pltpu.VMEM((5, 128, 128), F32), pltpu.VMEM((9, 48, 128), F32), pltpu.VMEM((LAYER, 128), F32)],
        name="coarse",
    )
    return level, grid


def solution(mesh):
    spec = P(AXES, None, None)
    return jax.shard_map(
        shards,
        mesh=mesh,
        in_specs=(spec, spec, spec, spec, spec, P()),
        out_specs=(spec, spec),
        check_vma=False,
    )
```

```python
import functools

import jax
import jax.numpy as jnp
from jax import lax
from jax.experimental import pallas as pl
from jax.experimental.pallas import tpu as pltpu
from jax.sharding import PartitionSpec as P

COLLECT_LIMIT = 56
AXES = ("wide", "narrow")
SPAN = 32
LAYER = 1024
SLOTS = 4
TILES = 4
F32 = jnp.float32
VMEM = pl.BlockSpec(memory_space=pltpu.VMEM)
SMEM = pl.BlockSpec(memory_space=pltpu.SMEM)
HBM = pl.BlockSpec(memory_space=pl.ANY)
FACES = jax.ShapeDtypeStruct((4, SPAN, 128), F32)
FIELD = jax.ShapeDtypeStruct((LAYER, 128), F32)
GHOSTS = pltpu.VMEM((4, SPAN, 128), F32)
PADDED = pltpu.VMEM((SPAN + 2, 48, 128), F32)


def lanes():
    return lax.broadcasted_iota(jnp.int32, (8, 128), 1)


def pick(tile, index):
    return jnp.take_along_axis(tile, index, axis=1, mode="promise_in_bounds")


def turned(tile, by):
    return pltpu.roll(tile, by, axis=1)


def part(xt):
    return pl.ds(8 * xt, 8)


def tile_row(y, zt):
    return pl.ds(pl.multiple_of(SPAN * y + 8 * zt, 8), 8)


def whereabouts(scalars):
    core = scalars[0]
    first, last = scalars[1], scalars[3]
    return core, jnp.where(core == 0, first, last - 4), last - first - 4


def positions(base):
    patch = base + lanes() // 32
    return patch % 2, (patch // 2) % 2, patch // 4


def put_faces(base, ref, faces):
    ix, iy, _ = positions(base)
    lane = lanes()
    for t in range(TILES):
        faces[0, part(t), :] = ref[pl.ds(256 * t, 8, stride=SPAN), :]
        faces[1, part(t), :] = ref[pl.ds(256 * t + 31, 8, stride=SPAN), :]
        faces[2, part(t), :] = jnp.where(iy == 1, ref[part(t), :], ref[pl.ds(31 * SPAN + 8 * t, 8), :])
    index = 32 * (lane // 32) + jnp.where(ix == 1, 0, 31)
    for t in range(TILES):
        found = pick(ref[part(t), :], index)
        for y in range(1, SPAN):
            found = jnp.where(lane % 32 == y, pick(ref[pl.ds(SPAN * y + 8 * t, 8), :], index), found)
        faces[3, part(t), :] = found


def ghosts(where, own, oth, far, post, out):
    core, base, extra = where
    lane = lanes()
    ix, iy, _ = positions(base)
    low = core == 0
    start = jnp.where(low, 4 - extra, extra)
    single = 1 if far is not None and len(far.shape) == 2 else 0
    x_far = jnp.where(low, 32, 64) + single
    x_post = jnp.where(low, 64, 32) + single
    x_turn = jnp.where(low, 96, 32)

    def mixer(turn, lift):
        target = (lane + turn) % 128
        index, index_post = (target + 32 * start) % 128, (target + 32 * start + lift) % 128
        here = jnp.where(target < 128 - 32 * start, 1, 0) == 1 - core
        if oth is None:
            return lambda a, b: jnp.zeros((8, 128), F32)
        return lambda a, b: jnp.where(here, pick(a, index), pick(b, index_post))

    mix_z, mix_y, mix_x = mixer(0, 0), mixer(64, single), mixer(128 - x_turn, x_post)
    y_index = (lane + 64 + single) % 128
    x_index = (lane + x_far + jnp.where(low, 96, 32)) % 128
    own_index = jnp.where(ix == 1, lane + 96, lane + 32) % 128
    for t in range(TILES):
        rows = part(t)
        if far is None:
            z_edge = y_edge = x_edge = 0.0
            z_post = nearest_post = None
        else:
            z_edge = far[rows, :] if single else far[0, rows, :]
            nearest = z_edge if single else far[1, rows, :]
            z_post = post[rows, :] if single else post[0, rows, :]
            nearest_post = z_post if single else post[1, rows, :]
            y_edge, x_edge = pick(nearest, y_index), pick(nearest, x_index)
        others = (None,) * 3 if oth is None else (oth[core, rows, :], oth[2, rows, :], oth[3, rows, :])
        mid = mix_z(others[0], z_post)
        out[0, rows, :], out[1, rows, :] = jnp.where(low, z_edge, mid), jnp.where(low, mid, z_edge)
        mid = mix_y(others[1], nearest_post)
        inner = turned(own[2, rows, :], 64)
        below, above = jnp.where(low, y_edge, mid), jnp.where(low, mid, y_edge)
        out[2, rows, :] = jnp.where(
            iy == 1, jnp.where(lane < 64, below, inner), jnp.where(lane < 64, inner, above)
        )
        mid = mix_x(others[2], nearest_post)
        inner = pick(own[3, rows, :], own_index)
        below, above = jnp.where(low, x_edge, mid), jnp.where(low, mid, x_edge)
        out[3, rows, :] = jnp.where(
            ix == 1, jnp.where(lane < 32, below, inner), jnp.where(lane >= 96, above, inner)
        )


def pad(base, ref, ghost, padded):
    _, iy, _ = positions(base)
    for t in range(TILES):
        rows = part(t)
        padded[0, 8 + 8 * t : 16 + 8 * t, :] = jnp.where(iy == 1, ghost[2, rows, :], 0.0)
        padded[SPAN + 1, 8 + 8 * t : 16 + 8 * t, :] = jnp.where(iy == 0, ghost[2, rows, :], 0.0)

    def layer(y, carry):
        for t in range(TILES):
            padded[y + 1, 8 + 8 * t : 16 + 8 * t, :] = ref[tile_row(y, t), :]
        padded[y + 1, 7:8, :] = ghost[0, pl.ds(y, 1), :]
        padded[y + 1, 40:41, :] = ghost[1, pl.ds(y, 1), :]
        return carry

    lax.fori_loop(0, SPAN, layer, 0, unroll=4)


def around(y, t, padded, ghost):
    lane = lanes()
    rows = slice(8 + 8 * t, 16 + 8 * t)
    own = padded[y + 1, rows, :]
    beyond = pick(ghost[3, part(t), :], 32 * (lane // 32) + y)
    return own, (
        jnp.where(lane % 32 == 0, beyond, turned(own, 1)),
        jnp.where(lane % 32 == 31, beyond, turned(own, 127)),
        padded[y, rows, :],
        padded[y + 2, rows, :],
        padded[y + 1, 7 + 8 * t : 15 + 8 * t, :],
        padded[y + 1, 9 + 8 * t : 17 + 8 * t, :],
    )


def parity(y):
    return (lax.broadcasted_iota(jnp.int32, (8, 128), 0) + lanes() + y) % 2


def inverted(x):
    guess = pl.reciprocal(x, approx=True)
    return guess * (2.0 - x * guess)


def collect_kernel(holder, v, k, kind, scalars, own, faces, bounds, hv, hk, hkind, sems):
    device = lax.axis_index(AXES)
    core = lax.rem(device, 2)
    landed = (hv, hk, hkind)
    copies = [pltpu.make_async_copy(ref, landed[i], sems.at[i]) for i, ref in enumerate((v, k, kind))]
    counting = pltpu.make_async_copy(holder, bounds, sems.at[3])
    counting.start()
    for copy in copies:
        copy.start()
    counting.wait()
    count = []
    for bound in (0, 1, 2, 4, 6):
        count.append(jnp.sum((bounds[...] < device - core + bound).astype(jnp.int32)))
        scalars[len(count)] = count[-1]
    scalars[0] = core
    base = jnp.where(core == 0, count[0], count[1])
    for i in range(3):
        copies[i].wait()
        for j in range(8):
            block = landed[i][:, pl.ds(128 * j, 128)].T
            if i == 2:
                block = 1.0 - 0.5 * block.astype(F32)
            own[i, pl.ds(128 * j, 128), :] = block
        put_faces(base, own.at[i], faces.at[pl.ds(4 * i, 4)])


def collect_rest_kernel(f, c, own, hf, hc, sems):
    landed = (hf, hc)
    copies = [pltpu.make_async_copy(ref, landed[i], sems.at[i]) for i, ref in enumerate((f, c))]
    for copy in copies:
        copy.start()
    for i in range(2):
        copies[i].wait()
        for j in range(8):
            own[i, pl.ds(128 * j, 128), :] = landed[i][:, pl.ds(128 * j, 128)].T


def window_of(scalars):
    core, extra = scalars[0], scalars[3] - scalars[1] - 4
    held = jnp.where(core == 0, scalars[2] - scalars[1], scalars[3] - scalars[2])
    lane = lanes()
    low = core == 0
    index = (lane + jnp.where(low, 0, 32 * held)) % 128
    index_other = (lane + jnp.where(low, 128 - 32 * held, 32 * extra)) % 128
    inside = (lane >= jnp.where(low, 0, 128 - 32 * held)) & (lane < jnp.where(low, 32 * held, 128))
    return lambda own, oth: jnp.where(inside, pick(own, index), pick(oth, index_other))


def face_window_kernel(scalars, own, oth, faces, sent):
    windowed = window_of(scalars)
    for i in range(12):
        for t in range(TILES):
            faces[i, part(t), :] = windowed(own[i, part(t), :], oth[i, part(t), :])
    put_sent(scalars, 1, faces, sent.at[0])
    for i in (1, 2):
        for t in range(TILES):
            z, nearest = outgoing(scalars, faces.at[pl.ds(4 * i, 4)], t, 0)
            sent[2 * i - 1, part(t), :] = z
            sent[2 * i, part(t), :] = nearest


def outgoing(scalars, faces, t, by):
    core = scalars[0]
    lane = (lanes() + 128 - by) % 128
    along_y = jnp.where(lane >= 64, 1, 0) == core
    y = faces[2, part(t), :]
    y = turned(y, by) if by else y
    x = pick(faces[3, part(t), :], (lane + 64 + 32 * core) % 128)
    return faces[core, part(t), :], jnp.where(along_y, y, x)


def put_sent(scalars, shade, faces, sent):
    mine = (lax.broadcasted_iota(jnp.int32, (8, 128), 0) + lanes() + scalars[0]) % 2 == shade
    for t in range(TILES):
        z, nearest = outgoing(scalars, faces, t, 1)
        sent[part(t), :] = jnp.where(mine, z, nearest)


def window_kernel(scalars, own, oth, own_rest, oth_rest, window, inner):
    windowed = window_of(scalars)
    for i in range(5):
        mine, theirs = (own.at[i], oth.at[i]) if i < 3 else (own_rest.at[i - 3], oth_rest.at[i - 3])

        def rows(y, carry):
            for t in range(TILES):
                at = tile_row(y, t)
                window[i, at, :] = windowed(mine[at, :], theirs[at, :])
            return carry

        lax.fori_loop(0, SPAN, rows, 0, unroll=8)

    row = lax.broadcasted_iota(jnp.int32, (8, 128), 0)

    def layer(y, carry):
        above = jnp.minimum(y + 1, SPAN - 1)
        heat = [window[1, tile_row(y, t), :] for t in range(TILES)]
        open_heat = [heat[t] * window[2, tile_row(y, t), :] for t in range(TILES)]
        heat_up = [pltpu.roll(x, 7, axis=0) for x in heat]
        open_up = [pltpu.roll(x, 7, axis=0) for x in open_heat]
        below = None
        for t in range(TILES):
            at = tile_row(y, t)
            doubled = 2.0 * open_heat[t]
            beside = doubled * turned(open_heat[t], 127) * inverted(heat[t] + turned(heat[t], 127))
            inner[0, at, :] = turned(beside, 1)
            inner[1, at, :] = beside
            heat2 = window[1, tile_row(above, t), :]
            inner[2, at, :] = doubled * window[2, tile_row(above, t), :] * heat2 * inverted(heat[t] + heat2)
            heat2, open2 = heat_up[t], open_up[t]
            if t < TILES - 1:
                heat2 = jnp.where(row == 7, heat_up[t + 1], heat2)
                open2 = jnp.where(row == 7, open_up[t + 1], open2)
            over = doubled * open2 * inverted(heat[t] + heat2)
            inner[4, at, :] = over
            lifted = pltpu.roll(over, 1, axis=0)
            inner[3, at, :] = lifted if below is None else jnp.where(row == 0, below, lifted)
            below = lifted
        return carry

    lax.fori_loop(0, SPAN, layer, 0, unroll=4)


def first_kernel(
    layers, scalars, fields, inner, own, oth, far, post, vo, fo, do, go, edge, faces, sent, ghost, pv, ends
):
    v, k, a, f, c = (fields.at[i] for i in range(5))
    where = whereabouts(scalars)
    base = where[1]
    ix, iy, iz = positions(base)
    lane = lanes()
    row = lax.broadcasted_iota(jnp.int32, (8, 128), 0)
    for number in range(3):
        group, outer = pl.ds(4 * number, 4), pl.ds(2 * number - 1, 2) if number else 0
        ghosts(where, own.at[group], oth.at[group], far.at[outer], post.at[outer], ghost.at[number])
    for t in range(TILES):
        rows = part(t)
        for face in range(4):
            heat, heat2 = own[4 + face, rows, :], ghost[1, face, rows, :]
            open_heat = heat * own[8 + face, rows, :]
            b = 2.0 * open_heat * ghost[2, face, rows, :] * heat2 * inverted(heat + heat2)
            edge[face, rows, :] = b
            if face < 2:
                ends[face, rows, :] = jnp.where(iz == (layers - 1 if face else 0), open_heat, b)
    pad(base, v, ghost.at[0], pv)
    low_in, low_out = (lane % 32 == 0) & (ix == 1), (lane % 32 == 0) & (ix == 0)
    high_in, high_out = (lane % 32 == 31) & (ix == 0), (lane % 32 == 31) & (ix == 1)

    def layer(y, carry):
        shade = parity(y)
        for t in range(TILES):
            rows = tile_row(y, t)
            value, values = around(y, t, pv, ghost.at[0])
            heat, opening = k[rows, :], a[rows, :]
            open_heat = heat * opening
            b_x = pick(edge[3, part(t), :], 32 * (lane // 32) + y)
            b_y = edge[2, part(t), :]
            b = [
                jnp.where(low_in, b_x, jnp.where(low_out, open_heat, inner[0, rows, :])),
                jnp.where(high_in, b_x, jnp.where(high_out, open_heat, inner[1, rows, :])),
                jnp.where(
                    y == 0, jnp.where(iy == 1, b_y, open_heat), inner[2, tile_row(jnp.maximum(y - 1, 0), t), :]
                ),
                jnp.where(y == SPAN - 1, jnp.where(iy == 0, b_y, open_heat), inner[2, rows, :]),
                inner[3, rows, :],
                inner[4, rows, :],
            ]
            if t == 0:
                b[4] = jnp.where(row == 0, ends[0, pl.ds(y, 1), :], b[4])
            if t == TILES - 1:
                b[5] = jnp.where(row == 7, ends[1, pl.ds(y, 1), :], b[5])
            summed = (b[0] + b[1]) + (b[2] + b[3]) + (b[4] + b[5])
            wall = jnp.where(opening == 0.5, heat, 0.0)
            diagonal = jnp.where(opening == 0.0, 1.0, c[rows, :] + summed + wall)
            inverse = inverted(diagonal)
            total = f[rows, :] * inverse
            fo[rows, :] = total
            do[rows, :] = diagonal
            b[0] = jnp.where(low_out, 0.0, b[0])
            b[1] = jnp.where(high_out, 0.0, b[1])
            for way in range(6):
                g = b[way] * inverse
                go[way, rows, :] = g
                total = total + g * values[way]
            vo[rows, :] = jnp.where(shade == 0, total, value)
        return carry

    lax.fori_loop(0, SPAN, layer, 0, unroll=16)
    put_faces(base, vo, faces)
    put_sent(scalars, 0, faces, sent)


def relaxed(y, t, f, g, padded, ghost):
    rows = tile_row(y, t)
    value, values = around(y, t, padded, ghost)
    total = f[rows, :]
    for way in range(6):
        total = total + g[way, rows, :] * values[way]
    return value, total


def sweep_kernel(shade_now, scalars, v, f, g, own, oth, far, post, vo, faces, *rest):
    *sent, ghost, padded = rest
    where = whereabouts(scalars)
    base = where[1]
    ghosts(where, own, oth, far, post, ghost)
    pad(base, v, ghost, padded)

    def layer(y, carry):
        shade = parity(y)
        for t in range(TILES):
            value, total = relaxed(y, t, f, g, padded, ghost)
            vo[tile_row(y, t), :] = jnp.where(shade == shade_now, total, value)
        return carry

    lax.fori_loop(0, SPAN, layer, 0, unroll=32)
    put_faces(base, vo, faces)
    if sent:
        put_sent(scalars, shade_now, faces, sent[0])


def residual_kernel(scalars, v, f, g, d, edge, own, blocks, cross, ghost, padded, pair):
    where = whereabouts(scalars)
    core = where[0]
    ghosts(where, own, None, None, None, ghost)
    pad(where[1], v, ghost, padded)
    lane = lanes()
    index = 2 * (lane % 64)

    def layer(y4, carry):
        for half in range(2):
            for t in range(TILES):
                added = None
                for step in range(2):
                    y = 4 * y4 + 2 * half + step
                    value, total = relaxed(y, t, f, g, padded, ghost)
                    rest = d[tile_row(y, t), :] * (total - value)
                    added = rest if added is None else added + rest
                pair[half, part(t), :] = added + turned(added, 127)
        for t in range(2):
            both = []
            for half in range(2):
                even = pair[half, pl.ds(16 * t, 8, stride=2), :]
                odd = pair[half, pl.ds(16 * t + 1, 8, stride=2), :]
                both.append(pick(even + odd, index))
            blocks[pl.ds(pl.multiple_of(16 * y4 + 8 * t, 8), 8), :] = (
                jnp.where(lane < 64, both[0], both[1]) * 0.125
            )
        return carry

    lax.fori_loop(0, 8, layer, 0, unroll=2)

    def pooled(face):
        for t in range(TILES):
            product = edge[face, part(t), :] * own[face, part(t), :]
            pair[0, part(t), :] = product + turned(product, 127)
        result = []
        for t in range(2):
            both = pair[0, pl.ds(16 * t, 8, stride=2), :] + pair[0, pl.ds(16 * t + 1, 8, stride=2), :]
            result.append(pick(both, index) * 0.125)
        return result

    for t, (z_low, z_high, along_y, along_x) in enumerate(zip(*(pooled(face) for face in range(4)))):
        blocks[128 + 8 * t : 136 + 8 * t, :] = z_low
        blocks[144 + 8 * t : 152 + 8 * t, :] = z_high
        blocks[160 + 8 * t : 168 + 8 * t, :] = jnp.where(lane < 64, along_y, along_x)
        cross[part(t), :] = jnp.where(core == 0, z_low, z_high)


def level_kernel(scalars, v, level, stack):
    core = scalars[0]
    held = jnp.where(core == 0, scalars[2] - scalars[1], scalars[3] - scalars[2])
    for j in range(8):
        stack[:, pl.ds(128 * j, 128)] = v[pl.ds(128 * j, 128), :].T
    for s in range(SLOTS):
        filled = s < held
        source = jnp.where(core == 0, s, jnp.where(filled, 4 - held + s, 0))
        for t in range(TILES):
            rows = pl.ds(pl.multiple_of(32 * source + 8 * t, 8), 8)
            level[s, part(t), :] = jnp.where(filled, stack[rows, :], 0.0)


def coarse_kernel(scalars, own, far, post, side, side_post, grid, table, crossing, joined):
    core = scalars[0]
    starts = [scalars[i] for i in (1, 3, 4, 5)]
    mine = jnp.where(core == 0, scalars[1], scalars[2])
    mine_end = jnp.where(core == 0, scalars[2], scalars[3])
    leader = lax.div(mine + 7, 8) * 8
    held = leader < mine_end
    low = core == 0
    lane = lanes()

    def child(patch):
        chip = (patch >= starts[1]).astype(jnp.int32) + (patch >= starts[2]).astype(jnp.int32)
        begin = jnp.where(chip == 0, starts[0], jnp.where(chip == 1, starts[1], starts[2]))
        end = jnp.where(chip == 0, starts[1], jnp.where(chip == 1, starts[2], starts[3]))
        return chip, patch - begin, end - begin

    def block(chip, j, count):
        entry = jnp.where(j < 4, j, j - count + 8)
        entry = jnp.clip(8 * chip + entry, 0, 19)
        return lax.div(entry, 4), lax.rem(entry, 4)

    @pl.when(held)
    def _():
        for t in range(16):
            rows = part(t)
            table[0, rows, :] = jnp.where(low, own[0, rows, :], own[1, rows, :])
            table[1, rows, :] = jnp.where(low, own[1, rows, :], own[0, rows, :])
            table[2, rows, :] = jnp.where(low, post[0, rows, :], far[0, rows, :])
            table[3, rows, :] = jnp.where(low, post[1, rows, :], far[1, rows, :])
            table[4, rows, :] = jnp.where(low, far[1, rows, :], post[1, rows, :])
        for t in range(6):
            rows, last = part(t), part(16 + t)
            crossing[2, rows, :] = jnp.where(low, own[0, last, :], own[1, last, :])
            crossing[3, rows, :] = jnp.where(low, own[1, last, :], own[0, last, :])
            crossing[4, rows, :] = jnp.where(low, post[0, last, :], far[0, last, :])
            crossing[5, rows, :] = jnp.where(low, post[1, last, :], far[1, last, :])
            crossing[6, rows, :] = jnp.where(low, far[1, last, :], post[1, last, :])
            crossing[7, rows, :] = jnp.where(low, far[0, last, :], post[0, last, :])
        for t in range(2):
            rows = part(t)
            crossing[1, part(2 + t), :] = jnp.where(low, side[rows, :], side_post[rows, :])
            crossing[8, rows, :] = jnp.where(low, side_post[rows, :], side[rows, :])

        def giver(chip, j, count, step):
            q = j + step
            in_first = j < 4
            begin = jnp.where(in_first, 0, count - 4)
            valid = (q < begin) | (q >= begin + 4)
            entry = 2 * chip + jnp.where(q < 0, 1, jnp.where(q >= count, 4, jnp.where(in_first, 3, 2)))
            slot = jnp.where(
                q < 0, q + 4, jnp.where(q >= count, q - count, jnp.where(in_first, q - count + 4, q))
            )
            return valid, jnp.clip(entry, 1, 8), slot

        def added(source, rows, index):
            valid, entry, slot = source
            return jnp.where(valid, pick(crossing[entry, rows, :], (index + 16 * slot) % 128), 0.0)

        for iy in range(2):
            for iz in range(2):
                left = child(leader + 2 * iy + 4 * iz)
                right = child(leader + 1 + 2 * iy + 4 * iz)
                left_block, left_slot = block(*left)
                right_block, right_slot = block(*right)
                for y in range(16):
                    for t in range(2):
                        rows = pl.ds(16 * (y // 2) + 8 * t, 8)
                        index = 64 * (y % 2) + lane % 16
                        a = pick(table[left_block, rows, :], index + 16 * left_slot)
                        b = pick(table[right_block, rows, :], index + 16 * right_slot)
                        joined[pl.ds(SPAN * (16 * iy + y) + 16 * iz + 8 * t, 8), :] = jnp.where(lane < 16, a, b)

                def pair_of(step, rows):
                    tiles = [added(giver(*one, step), rows, lane % 16) for one in (left, right)]
                    return jnp.where(lane < 16, tiles[0], tiles[1])

                first_row = SPAN * 16 * iy + 16 * iz
                for t in range(2):
                    at = pl.ds(first_row + 8 * SPAN * t, 8, stride=SPAN)
                    joined[at, :] = joined[at, :] + pair_of(-4, part(2 + t))
                    at = pl.ds(first_row + 8 * SPAN * t + 15, 8, stride=SPAN)
                    joined[at, :] = joined[at, :] + pair_of(4, part(t))
                    at = pl.ds(first_row + (0 if iy else 15 * SPAN) + 8 * t, 8)
                    joined[at, :] = joined[at, :] + pair_of(-2 if iy else 2, part(4 + t))
                from_right, from_left = giver(*left, 1), giver(*right, -1)

                @pl.when(from_right[0] | from_left[0])
                def _():
                    for y in range(16):
                        for t in range(2):
                            at = pl.ds(first_row + SPAN * y + 8 * t, 8)
                            high = added(from_right, part(4 + t), 0 * lane + 64 + y)
                            low_side = added(from_left, part(4 + t), 0 * lane + 64 + y)
                            side_tile = jnp.where(lane == 15, high, jnp.where(lane == 16, low_side, 0.0))
                            joined[at, :] = joined[at, :] + side_tile

        for j in range(8):
            turn = joined[pl.ds(128 * j, 128), :].T
            grid[0, :, pl.ds(128 * j, 128)] = turn[0:SPAN, :]

    @pl.when(jnp.logical_not(held))
    def _():
        grid[0] = jnp.zeros((SPAN, LAYER), F32)


def call(kernel, out_shape, operands, specs=None, out_specs=None, scratch=(), name=None, limit=32, leading=(SMEM,)):
    return pl.pallas_call(
        kernel,
        out_shape=out_shape,
        in_specs=list(leading) + (specs or [VMEM] * (len(operands) - 1)),
        out_specs=out_specs or jax.tree.map(lambda _: VMEM, out_shape),
        scratch_shapes=list(scratch),
        compiler_params=pltpu.CompilerParams(vmem_limit_bytes=limit * 1024 * 1024),
        name=name,
    )(*operands)


def shards(v, f, k, c, kind, holder):
    devices = lax.axis_size(AXES)
    swap = [(i, i ^ 1) for i in range(devices)]
    reach = [(i, i + 1) for i in range(1, devices - 1, 2)]
    reach = reach + [(b, a) for a, b in reach]
    patches = holder.shape[0]

    def exchange(faces, sent):
        far = lax.ppermute(sent, AXES, reach)
        oth = lax.ppermute(faces, AXES, swap)
        post = lax.ppermute(far, AXES, swap)
        return faces, oth, far, post

    v, f, k, c, kind = (x.reshape(SLOTS * SPAN, LAYER) for x in (v, f, k, c, kind))
    five = jax.ShapeDtypeStruct((5, LAYER, 128), F32)
    twelve = jax.ShapeDtypeStruct((12, SPAN, 128), F32)
    sent_first = jax.ShapeDtypeStruct((5, SPAN, 128), F32)
    sent_later = jax.ShapeDtypeStruct((SPAN, 128), F32)
    landing = pltpu.VMEM((SLOTS * SPAN, LAYER), F32)
    scalars, own, faces = call(
        collect_kernel,
        [pltpu.SMEM((6,), jnp.int32), pltpu.VMEM((3, LAYER, 128), F32), pltpu.VMEM(twelve.shape, F32)],
        [holder.reshape(patches // 128, 128), v, k, kind],
        specs=[HBM] * 4,
        leading=[],
        out_specs=[SMEM, VMEM, VMEM],
        scratch=[pltpu.VMEM((patches // 128, 128), jnp.int32), landing, landing]
        + [pltpu.VMEM((SLOTS * SPAN, LAYER), jnp.int32), pltpu.SemaphoreType.DMA((4,))],
        name="collect",
        limit=COLLECT_LIMIT,
    )
    own_rest = call(
        collect_rest_kernel,
        pltpu.VMEM((2, LAYER, 128), F32),
        [f, c],
        specs=[HBM] * 2,
        leading=[],
        out_specs=VMEM,
        scratch=[landing, landing, pltpu.SemaphoreType.DMA((2,))],
        name="collect_rest",
        limit=COLLECT_LIMIT,
    )
    oth, own_rest = lax.optimization_barrier((lax.ppermute(faces, AXES, swap), own_rest))
    faces, sent = call(
        face_window_kernel,
        [twelve, sent_first],
        [scalars, faces, oth],
        name="face_window",
    )
    sent, own, own_rest = lax.optimization_barrier((sent, own, own_rest))
    far = lax.ppermute(sent, AXES, reach)
    oth = lax.ppermute(faces, AXES, swap)
    window, inner = call(
        window_kernel,
        [five, five],
        [scalars, own, lax.ppermute(own, AXES, swap), own_rest, lax.ppermute(own_rest, AXES, swap)],
        name="window",
    )
    far, window, inner = lax.optimization_barrier((far, window, inner))
    post = lax.ppermute(far, AXES, swap)
    coefficients = jax.ShapeDtypeStruct((6, LAYER, 128), F32)
    wv, wf, wd, wg, edge, faces, *sent = call(
        functools.partial(first_kernel, patches // 4),
        [FIELD, FIELD, FIELD, coefficients, FACES, FACES, sent_later],
        [scalars, window, inner, faces, oth, far, post],
        scratch=[pltpu.VMEM((3, 4, SPAN, 128), F32), PADDED, pltpu.VMEM((2, SPAN, 128), F32)],
        name="first",
    )
    for shade, more in ((1, [sent_later]), (0, [sent_later]), (1, [])):
        wv, faces, *sent = call(
            functools.partial(sweep_kernel, shade),
            [FIELD, FACES] + more,
            [scalars, wv, wf, wg, *exchange(faces, *sent)],
            scratch=[GHOSTS, PADDED],
            name="sweep",
        )
    blocks, cross = call(
        residual_kernel,
        [jax.ShapeDtypeStruct((176, 128), F32), jax.ShapeDtypeStruct((16, 128), F32)],
        [scalars, wv, wf, wg, wd, edge, faces],
        scratch=[GHOSTS, PADDED, pltpu.VMEM((2, SPAN, 128), F32)],
        name="residual",
    )
    beside = [(i, i - 5) for i in range(6, devices, 2)] + [(i, i + 1) for i in range(1, devices - 1, 2)]
    both = jnp.stack([blocks, lax.ppermute(blocks, AXES, swap)], 0)
    downward = [(i, i - 1) for i in range(2, devices, 2)] + [(i, i - 5) for i in range(5, devices, 2)]
    far = lax.ppermute(both, AXES, downward)
    side = lax.ppermute(cross, AXES, beside)
    far, wv = lax.optimization_barrier((far, wv))
    level = call(
        level_kernel,
        jax.ShapeDtypeStruct((SLOTS, SPAN, LAYER), F32),
        [scalars, wv],
        scratch=[pltpu.VMEM((128, LAYER), F32)],
        name="level",
    )
    side, level = lax.optimization_barrier((side, level))
    side, far = lax.optimization_barrier((side, far))
    post = lax.ppermute(far, AXES, swap)
    side_post = lax.ppermute(side, AXES, swap)
    grid = call(
        coarse_kernel,
        jax.ShapeDtypeStruct((1, SPAN, LAYER), F32),
        [scalars, both, far, post, side, side_post],
        scratch=[pltpu.VMEM((5, 128, 128), F32), pltpu.VMEM((9, 48, 128), F32), pltpu.VMEM((LAYER, 128), F32)],
        name="coarse",
    )
    return level, grid


def solution(mesh):
    spec = P(AXES, None, None)
    return jax.shard_map(
        shards,
        mesh=mesh,
        in_specs=(spec, spec, spec, spec, spec, P()),
        out_specs=(spec, spec),
        check_vma=False,
    )
```

```python
import functools

import jax
import jax.numpy as jnp
from jax import lax
from jax.experimental import pallas as pl
from jax.experimental.pallas import tpu as pltpu
from jax.sharding import PartitionSpec as P

COLLECT_LIMIT = 56
AXES = ("wide", "narrow")
SPAN = 32
LAYER = 1024
SLOTS = 4
TILES = 4
F32 = jnp.float32
VMEM = pl.BlockSpec(memory_space=pltpu.VMEM)
SMEM = pl.BlockSpec(memory_space=pltpu.SMEM)
HBM = pl.BlockSpec(memory_space=pl.ANY)
FACES = jax.ShapeDtypeStruct((4, SPAN, 128), F32)
FIELD = jax.ShapeDtypeStruct((LAYER, 128), F32)
GHOSTS = pltpu.VMEM((4, SPAN, 128), F32)
PADDED = pltpu.VMEM((SPAN + 2, 48, 128), F32)


def lanes():
    return lax.broadcasted_iota(jnp.int32, (8, 128), 1)


def pick(tile, index):
    return jnp.take_along_axis(tile, index, axis=1, mode="promise_in_bounds")


def turned(tile, by):
    return pltpu.roll(tile, by, axis=1)


def part(xt):
    return pl.ds(8 * xt, 8)


def tile_row(y, zt):
    return pl.ds(pl.multiple_of(SPAN * y + 8 * zt, 8), 8)


def whereabouts(scalars):
    core = scalars[0]
    first, last = scalars[1], scalars[3]
    return core, jnp.where(core == 0, first, last - 4), last - first - 4


def positions(base):
    patch = base + lanes() // 32
    return patch % 2, (patch // 2) % 2, patch // 4


def put_faces(base, ref, faces):
    ix, iy, _ = positions(base)
    lane = lanes()
    for t in range(TILES):
        faces[0, part(t), :] = ref[pl.ds(256 * t, 8, stride=SPAN), :]
        faces[1, part(t), :] = ref[pl.ds(256 * t + 31, 8, stride=SPAN), :]
        faces[2, part(t), :] = jnp.where(iy == 1, ref[part(t), :], ref[pl.ds(31 * SPAN + 8 * t, 8), :])
    index = 32 * (lane // 32) + jnp.where(ix == 1, 0, 31)
    for t in range(TILES):
        found = pick(ref[part(t), :], index)
        for y in range(1, SPAN):
            found = jnp.where(lane % 32 == y, pick(ref[pl.ds(SPAN * y + 8 * t, 8), :], index), found)
        faces[3, part(t), :] = found


def ghosts(where, own, oth, far, post, out):
    core, base, extra = where
    lane = lanes()
    ix, iy, _ = positions(base)
    low = core == 0
    start = jnp.where(low, 4 - extra, extra)
    single = 1 if far is not None and len(far.shape) == 2 else 0
    x_far = jnp.where(low, 32, 64) + single
    x_post = jnp.where(low, 64, 32) + single
    x_turn = jnp.where(low, 96, 32)

    def mixer(turn, lift):
        target = (lane + turn) % 128
        index, index_post = (target + 32 * start) % 128, (target + 32 * start + lift) % 128
        here = jnp.where(target < 128 - 32 * start, 1, 0) == 1 - core
        if oth is None:
            return lambda a, b: jnp.zeros((8, 128), F32)
        return lambda a, b: jnp.where(here, pick(a, index), pick(b, index_post))

    mix_z, mix_y, mix_x = mixer(0, 0), mixer(64, single), mixer(128 - x_turn, x_post)
    y_index = (lane + 64 + single) % 128
    x_index = (lane + x_far + jnp.where(low, 96, 32)) % 128
    own_index = jnp.where(ix == 1, lane + 96, lane + 32) % 128
    for t in range(TILES):
        rows = part(t)
        if far is None:
            z_edge = y_edge = x_edge = 0.0
            z_post = nearest_post = None
        else:
            z_edge = far[rows, :] if single else far[0, rows, :]
            nearest = z_edge if single else far[1, rows, :]
            z_post = post[rows, :] if single else post[0, rows, :]
            nearest_post = z_post if single else post[1, rows, :]
            y_edge, x_edge = pick(nearest, y_index), pick(nearest, x_index)
        others = (None,) * 3 if oth is None else (oth[core, rows, :], oth[2, rows, :], oth[3, rows, :])
        mid = mix_z(others[0], z_post)
        out[0, rows, :], out[1, rows, :] = jnp.where(low, z_edge, mid), jnp.where(low, mid, z_edge)
        mid = mix_y(others[1], nearest_post)
        inner = turned(own[2, rows, :], 64)
        below, above = jnp.where(low, y_edge, mid), jnp.where(low, mid, y_edge)
        out[2, rows, :] = jnp.where(
            iy == 1, jnp.where(lane < 64, below, inner), jnp.where(lane < 64, inner, above)
        )
        mid = mix_x(others[2], nearest_post)
        inner = pick(own[3, rows, :], own_index)
        below, above = jnp.where(low, x_edge, mid), jnp.where(low, mid, x_edge)
        out[3, rows, :] = jnp.where(
            ix == 1, jnp.where(lane < 32, below, inner), jnp.where(lane >= 96, above, inner)
        )


def pad(base, ref, ghost, padded):
    _, iy, _ = positions(base)
    for t in range(TILES):
        rows = part(t)
        padded[0, 8 + 8 * t : 16 + 8 * t, :] = jnp.where(iy == 1, ghost[2, rows, :], 0.0)
        padded[SPAN + 1, 8 + 8 * t : 16 + 8 * t, :] = jnp.where(iy == 0, ghost[2, rows, :], 0.0)

    def layer(y, carry):
        for t in range(TILES):
            padded[y + 1, 8 + 8 * t : 16 + 8 * t, :] = ref[tile_row(y, t), :]
        padded[y + 1, 7:8, :] = ghost[0, pl.ds(y, 1), :]
        padded[y + 1, 40:41, :] = ghost[1, pl.ds(y, 1), :]
        return carry

    lax.fori_loop(0, SPAN, layer, 0, unroll=16)


def around(y, t, padded, ghost):
    lane = lanes()
    rows = slice(8 + 8 * t, 16 + 8 * t)
    own = padded[y + 1, rows, :]
    beyond = pick(ghost[3, part(t), :], 32 * (lane // 32) + y)
    return own, (
        jnp.where(lane % 32 == 0, beyond, turned(own, 1)),
        jnp.where(lane % 32 == 31, beyond, turned(own, 127)),
        padded[y, rows, :],
        padded[y + 2, rows, :],
        padded[y + 1, 7 + 8 * t : 15 + 8 * t, :],
        padded[y + 1, 9 + 8 * t : 17 + 8 * t, :],
    )


def parity(y):
    return (lax.broadcasted_iota(jnp.int32, (8, 128), 0) + lanes() + y) % 2


def inverted(x):
    guess = pl.reciprocal(x, approx=True)
    return guess * (2.0 - x * guess)


def collect_kernel(holder, v, k, kind, scalars, own, faces, bounds, hv, hk, hkind, sems):
    device = lax.axis_index(AXES)
    core = lax.rem(device, 2)
    landed = (hv, hk, hkind)
    copies = [pltpu.make_async_copy(ref, landed[i], sems.at[i]) for i, ref in enumerate((v, k, kind))]
    counting = pltpu.make_async_copy(holder, bounds, sems.at[3])
    counting.start()
    for copy in copies:
        copy.start()
    counting.wait()
    count = []
    for bound in (0, 1, 2, 4, 6):
        count.append(jnp.sum((bounds[...] < device - core + bound).astype(jnp.int32)))
        scalars[len(count)] = count[-1]
    scalars[0] = core
    base = jnp.where(core == 0, count[0], count[1])
    for i in range(3):
        copies[i].wait()
        for j in range(8):
            block = landed[i][:, pl.ds(128 * j, 128)].T
            if i == 2:
                block = 1.0 - 0.5 * block.astype(F32)
            own[i, pl.ds(128 * j, 128), :] = block
        put_faces(base, own.at[i], faces.at[pl.ds(4 * i, 4)])


def collect_rest_kernel(f, c, own, hf, hc, sems):
    landed = (hf, hc)
    copies = [pltpu.make_async_copy(ref, landed[i], sems.at[i]) for i, ref in enumerate((f, c))]
    for copy in copies:
        copy.start()
    for i in range(2):
        copies[i].wait()
        for j in range(8):
            own[i, pl.ds(128 * j, 128), :] = landed[i][:, pl.ds(128 * j, 128)].T


def window_of(scalars):
    core, extra = scalars[0], scalars[3] - scalars[1] - 4
    held = jnp.where(core == 0, scalars[2] - scalars[1], scalars[3] - scalars[2])
    lane = lanes()
    low = core == 0
    index = (lane + jnp.where(low, 0, 32 * held)) % 128
    index_other = (lane + jnp.where(low, 128 - 32 * held, 32 * extra)) % 128
    inside = (lane >= jnp.where(low, 0, 128 - 32 * held)) & (lane < jnp.where(low, 32 * held, 128))
    return lambda own, oth: jnp.where(inside, pick(own, index), pick(oth, index_other))


def face_window_kernel(scalars, own, oth, faces, sent):
    windowed = window_of(scalars)
    for i in range(12):
        for t in range(TILES):
            faces[i, part(t), :] = windowed(own[i, part(t), :], oth[i, part(t), :])
    put_sent(scalars, 1, faces, sent.at[0])
    for i in (1, 2):
        for t in range(TILES):
            z, nearest = outgoing(scalars, faces.at[pl.ds(4 * i, 4)], t, 0)
            sent[2 * i - 1, part(t), :] = z
            sent[2 * i, part(t), :] = nearest


def outgoing(scalars, faces, t, by):
    core = scalars[0]
    lane = (lanes() + 128 - by) % 128
    along_y = jnp.where(lane >= 64, 1, 0) == core
    y = faces[2, part(t), :]
    y = turned(y, by) if by else y
    x = pick(faces[3, part(t), :], (lane + 64 + 32 * core) % 128)
    return faces[core, part(t), :], jnp.where(along_y, y, x)


def put_sent(scalars, shade, faces, sent):
    mine = (lax.broadcasted_iota(jnp.int32, (8, 128), 0) + lanes() + scalars[0]) % 2 == shade
    for t in range(TILES):
        z, nearest = outgoing(scalars, faces, t, 1)
        sent[part(t), :] = jnp.where(mine, z, nearest)


def window_kernel(scalars, own, oth, own_rest, oth_rest, window, inner):
    windowed = window_of(scalars)
    for i in range(5):
        mine, theirs = (own.at[i], oth.at[i]) if i < 3 else (own_rest.at[i - 3], oth_rest.at[i - 3])

        def rows(y, carry):
            for t in range(TILES):
                at = tile_row(y, t)
                window[i, at, :] = windowed(mine[at, :], theirs[at, :])
            return carry

        lax.fori_loop(0, SPAN, rows, 0, unroll=8)

    row = lax.broadcasted_iota(jnp.int32, (8, 128), 0)

    def layer(y, carry):
        above = jnp.minimum(y + 1, SPAN - 1)
        heat = [window[1, tile_row(y, t), :] for t in range(TILES)]
        open_heat = [heat[t] * window[2, tile_row(y, t), :] for t in range(TILES)]
        heat_up = [pltpu.roll(x, 7, axis=0) for x in heat]
        open_up = [pltpu.roll(x, 7, axis=0) for x in open_heat]
        below = None
        for t in range(TILES):
            at = tile_row(y, t)
            doubled = 2.0 * open_heat[t]
            beside = doubled * turned(open_heat[t], 127) * inverted(heat[t] + turned(heat[t], 127))
            inner[0, at, :] = turned(beside, 1)
            inner[1, at, :] = beside
            heat2 = window[1, tile_row(above, t), :]
            inner[2, at, :] = doubled * window[2, tile_row(above, t), :] * heat2 * inverted(heat[t] + heat2)
            heat2, open2 = heat_up[t], open_up[t]
            if t < TILES - 1:
                heat2 = jnp.where(row == 7, heat_up[t + 1], heat2)
                open2 = jnp.where(row == 7, open_up[t + 1], open2)
            over = doubled * open2 * inverted(heat[t] + heat2)
            inner[4, at, :] = over
            lifted = pltpu.roll(over, 1, axis=0)
            inner[3, at, :] = lifted if below is None else jnp.where(row == 0, below, lifted)
            below = lifted
        return carry

    lax.fori_loop(0, SPAN, layer, 0, unroll=4)


def first_kernel(
    layers, scalars, fields, inner, own, oth, far, post, vo, fo, do, go, edge, faces, sent, ghost, pv, ends
):
    v, k, a, f, c = (fields.at[i] for i in range(5))
    where = whereabouts(scalars)
    base = where[1]
    ix, iy, iz = positions(base)
    lane = lanes()
    row = lax.broadcasted_iota(jnp.int32, (8, 128), 0)
    for number in range(3):
        group, outer = pl.ds(4 * number, 4), pl.ds(2 * number - 1, 2) if number else 0
        ghosts(where, own.at[group], oth.at[group], far.at[outer], post.at[outer], ghost.at[number])
    for t in range(TILES):
        rows = part(t)
        for face in range(4):
            heat, heat2 = own[4 + face, rows, :], ghost[1, face, rows, :]
            open_heat = heat * own[8 + face, rows, :]
            b = 2.0 * open_heat * ghost[2, face, rows, :] * heat2 * inverted(heat + heat2)
            edge[face, rows, :] = b
            if face < 2:
                ends[face, rows, :] = jnp.where(iz == (layers - 1 if face else 0), open_heat, b)
    pad(base, v, ghost.at[0], pv)
    low_in, low_out = (lane % 32 == 0) & (ix == 1), (lane % 32 == 0) & (ix == 0)
    high_in, high_out = (lane % 32 == 31) & (ix == 0), (lane % 32 == 31) & (ix == 1)

    def layer(y, carry):
        shade = parity(y)
        for t in range(TILES):
            rows = tile_row(y, t)
            value, values = around(y, t, pv, ghost.at[0])
            heat, opening = k[rows, :], a[rows, :]
            open_heat = heat * opening
            b_x = pick(edge[3, part(t), :], 32 * (lane // 32) + y)
            b_y = edge[2, part(t), :]
            b = [
                jnp.where(low_in, b_x, jnp.where(low_out, open_heat, inner[0, rows, :])),
                jnp.where(high_in, b_x, jnp.where(high_out, open_heat, inner[1, rows, :])),
                jnp.where(
                    y == 0, jnp.where(iy == 1, b_y, open_heat), inner[2, tile_row(jnp.maximum(y - 1, 0), t), :]
                ),
                jnp.where(y == SPAN - 1, jnp.where(iy == 0, b_y, open_heat), inner[2, rows, :]),
                inner[3, rows, :],
                inner[4, rows, :],
            ]
            if t == 0:
                b[4] = jnp.where(row == 0, ends[0, pl.ds(y, 1), :], b[4])
            if t == TILES - 1:
                b[5] = jnp.where(row == 7, ends[1, pl.ds(y, 1), :], b[5])
            summed = (b[0] + b[1]) + (b[2] + b[3]) + (b[4] + b[5])
            wall = jnp.where(opening == 0.5, heat, 0.0)
            diagonal = jnp.where(opening == 0.0, 1.0, c[rows, :] + summed + wall)
            inverse = inverted(diagonal)
            total = f[rows, :] * inverse
            fo[rows, :] = total
            do[rows, :] = diagonal
            b[0] = jnp.where(low_out, 0.0, b[0])
            b[1] = jnp.where(high_out, 0.0, b[1])
            for way in range(6):
                g = b[way] * inverse
                go[way, rows, :] = g
                total = total + g * values[way]
            vo[rows, :] = jnp.where(shade == 0, total, value)
        return carry

    lax.fori_loop(0, SPAN, layer, 0, unroll=16)
    put_faces(base, vo, faces)
    put_sent(scalars, 0, faces, sent)


def relaxed(y, t, f, g, padded, ghost):
    rows = tile_row(y, t)
    value, values = around(y, t, padded, ghost)
    total = f[rows, :]
    for way in range(6):
        total = total + g[way, rows, :] * values[way]
    return value, total


def sweep_kernel(shade_now, scalars, v, f, g, own, oth, far, post, vo, faces, *rest):
    *sent, ghost, padded = rest
    where = whereabouts(scalars)
    base = where[1]
    ghosts(where, own, oth, far, post, ghost)
    pad(base, v, ghost, padded)

    def layer(y, carry):
        shade = parity(y)
        for t in range(TILES):
            value, total = relaxed(y, t, f, g, padded, ghost)
            vo[tile_row(y, t), :] = jnp.where(shade == shade_now, total, value)
        return carry

    lax.fori_loop(0, SPAN, layer, 0, unroll=32)
    put_faces(base, vo, faces)
    if sent:
        put_sent(scalars, shade_now, faces, sent[0])


def residual_kernel(scalars, v, f, g, d, edge, own, blocks, cross, ghost, padded, pair):
    where = whereabouts(scalars)
    core = where[0]
    ghosts(where, own, None, None, None, ghost)
    pad(where[1], v, ghost, padded)
    lane = lanes()
    index = 2 * (lane % 64)

    def layer(y4, carry):
        for half in range(2):
            for t in range(TILES):
                added = None
                for step in range(2):
                    y = 4 * y4 + 2 * half + step
                    value, total = relaxed(y, t, f, g, padded, ghost)
                    rest = d[tile_row(y, t), :] * (total - value)
                    added = rest if added is None else added + rest
                pair[half, part(t), :] = added + turned(added, 127)
        for t in range(2):
            both = []
            for half in range(2):
                even = pair[half, pl.ds(16 * t, 8, stride=2), :]
                odd = pair[half, pl.ds(16 * t + 1, 8, stride=2), :]
                both.append(pick(even + odd, index))
            blocks[pl.ds(pl.multiple_of(16 * y4 + 8 * t, 8), 8), :] = (
                jnp.where(lane < 64, both[0], both[1]) * 0.125
            )
        return carry

    lax.fori_loop(0, 8, layer, 0, unroll=2)

    def pooled(face):
        for t in range(TILES):
            product = edge[face, part(t), :] * own[face, part(t), :]
            pair[0, part(t), :] = product + turned(product, 127)
        result = []
        for t in range(2):
            both = pair[0, pl.ds(16 * t, 8, stride=2), :] + pair[0, pl.ds(16 * t + 1, 8, stride=2), :]
            result.append(pick(both, index) * 0.125)
        return result

    for t, (z_low, z_high, along_y, along_x) in enumerate(zip(*(pooled(face) for face in range(4)))):
        blocks[128 + 8 * t : 136 + 8 * t, :] = z_low
        blocks[144 + 8 * t : 152 + 8 * t, :] = z_high
        blocks[160 + 8 * t : 168 + 8 * t, :] = jnp.where(lane < 64, along_y, along_x)
        cross[part(t), :] = jnp.where(core == 0, z_low, z_high)


def level_kernel(scalars, v, level, stack):
    core = scalars[0]
    held = jnp.where(core == 0, scalars[2] - scalars[1], scalars[3] - scalars[2])
    for j in range(8):
        stack[:, pl.ds(128 * j, 128)] = v[pl.ds(128 * j, 128), :].T
    for s in range(SLOTS):
        filled = s < held
        source = jnp.where(core == 0, s, jnp.where(filled, 4 - held + s, 0))
        for t in range(TILES):
            rows = pl.ds(pl.multiple_of(32 * source + 8 * t, 8), 8)
            level[s, part(t), :] = jnp.where(filled, stack[rows, :], 0.0)


def coarse_kernel(scalars, own, far, post, side, side_post, grid, table, crossing, joined):
    core = scalars[0]
    starts = [scalars[i] for i in (1, 3, 4, 5)]
    mine = jnp.where(core == 0, scalars[1], scalars[2])
    mine_end = jnp.where(core == 0, scalars[2], scalars[3])
    leader = lax.div(mine + 7, 8) * 8
    held = leader < mine_end
    low = core == 0
    lane = lanes()

    def child(patch):
        chip = (patch >= starts[1]).astype(jnp.int32) + (patch >= starts[2]).astype(jnp.int32)
        begin = jnp.where(chip == 0, starts[0], jnp.where(chip == 1, starts[1], starts[2]))
        end = jnp.where(chip == 0, starts[1], jnp.where(chip == 1, starts[2], starts[3]))
        return chip, patch - begin, end - begin

    def block(chip, j, count):
        entry = jnp.where(j < 4, j, j - count + 8)
        entry = jnp.clip(8 * chip + entry, 0, 19)
        return lax.div(entry, 4), lax.rem(entry, 4)

    @pl.when(held)
    def _():
        for t in range(16):
            rows = part(t)
            table[0, rows, :] = jnp.where(low, own[0, rows, :], own[1, rows, :])
            table[1, rows, :] = jnp.where(low, own[1, rows, :], own[0, rows, :])
            table[2, rows, :] = jnp.where(low, post[0, rows, :], far[0, rows, :])
            table[3, rows, :] = jnp.where(low, post[1, rows, :], far[1, rows, :])
            table[4, rows, :] = jnp.where(low, far[1, rows, :], post[1, rows, :])
        for t in range(6):
            rows, last = part(t), part(16 + t)
            crossing[2, rows, :] = jnp.where(low, own[0, last, :], own[1, last, :])
            crossing[3, rows, :] = jnp.where(low, own[1, last, :], own[0, last, :])
            crossing[4, rows, :] = jnp.where(low, post[0, last, :], far[0, last, :])
            crossing[5, rows, :] = jnp.where(low, post[1, last, :], far[1, last, :])
            crossing[6, rows, :] = jnp.where(low, far[1, last, :], post[1, last, :])
            crossing[7, rows, :] = jnp.where(low, far[0, last, :], post[0, last, :])
        for t in range(2):
            rows = part(t)
            crossing[1, part(2 + t), :] = jnp.where(low, side[rows, :], side_post[rows, :])
            crossing[8, rows, :] = jnp.where(low, side_post[rows, :], side[rows, :])

        def giver(chip, j, count, step):
            q = j + step
            in_first = j < 4
            begin = jnp.where(in_first, 0, count - 4)
            valid = (q < begin) | (q >= begin + 4)
            entry = 2 * chip + jnp.where(q < 0, 1, jnp.where(q >= count, 4, jnp.where(in_first, 3, 2)))
            slot = jnp.where(
                q < 0, q + 4, jnp.where(q >= count, q - count, jnp.where(in_first, q - count + 4, q))
            )
            return valid, jnp.clip(entry, 1, 8), slot

        def added(source, rows, index):
            valid, entry, slot = source
            return jnp.where(valid, pick(crossing[entry, rows, :], (index + 16 * slot) % 128), 0.0)

        for iy in range(2):
            for iz in range(2):
                left = child(leader + 2 * iy + 4 * iz)
                right = child(leader + 1 + 2 * iy + 4 * iz)
                left_block, left_slot = block(*left)
                right_block, right_slot = block(*right)
                for y in range(16):
                    for t in range(2):
                        rows = pl.ds(16 * (y // 2) + 8 * t, 8)
                        index = 64 * (y % 2) + lane % 16
                        a = pick(table[left_block, rows, :], index + 16 * left_slot)
                        b = pick(table[right_block, rows, :], index + 16 * right_slot)
                        joined[pl.ds(SPAN * (16 * iy + y) + 16 * iz + 8 * t, 8), :] = jnp.where(lane < 16, a, b)

                def pair_of(step, rows):
                    tiles = [added(giver(*one, step), rows, lane % 16) for one in (left, right)]
                    return jnp.where(lane < 16, tiles[0], tiles[1])

                first_row = SPAN * 16 * iy + 16 * iz
                for t in range(2):
                    at = pl.ds(first_row + 8 * SPAN * t, 8, stride=SPAN)
                    joined[at, :] = joined[at, :] + pair_of(-4, part(2 + t))
                    at = pl.ds(first_row + 8 * SPAN * t + 15, 8, stride=SPAN)
                    joined[at, :] = joined[at, :] + pair_of(4, part(t))
                    at = pl.ds(first_row + (0 if iy else 15 * SPAN) + 8 * t, 8)
                    joined[at, :] = joined[at, :] + pair_of(-2 if iy else 2, part(4 + t))
                from_right, from_left = giver(*left, 1), giver(*right, -1)

                @pl.when(from_right[0] | from_left[0])
                def _():
                    for y in range(16):
                        for t in range(2):
                            at = pl.ds(first_row + SPAN * y + 8 * t, 8)
                            high = added(from_right, part(4 + t), 0 * lane + 64 + y)
                            low_side = added(from_left, part(4 + t), 0 * lane + 64 + y)
                            side_tile = jnp.where(lane == 15, high, jnp.where(lane == 16, low_side, 0.0))
                            joined[at, :] = joined[at, :] + side_tile

        for j in range(8):
            turn = joined[pl.ds(128 * j, 128), :].T
            grid[0, :, pl.ds(128 * j, 128)] = turn[0:SPAN, :]

    @pl.when(jnp.logical_not(held))
    def _():
        grid[0] = jnp.zeros((SPAN, LAYER), F32)


def call(kernel, out_shape, operands, specs=None, out_specs=None, scratch=(), name=None, limit=32, leading=(SMEM,)):
    return pl.pallas_call(
        kernel,
        out_shape=out_shape,
        in_specs=list(leading) + (specs or [VMEM] * (len(operands) - 1)),
        out_specs=out_specs or jax.tree.map(lambda _: VMEM, out_shape),
        scratch_shapes=list(scratch),
        compiler_params=pltpu.CompilerParams(vmem_limit_bytes=limit * 1024 * 1024),
        name=name,
    )(*operands)


def shards(v, f, k, c, kind, holder):
    devices = lax.axis_size(AXES)
    swap = [(i, i ^ 1) for i in range(devices)]
    reach = [(i, i + 1) for i in range(1, devices - 1, 2)]
    reach = reach + [(b, a) for a, b in reach]
    patches = holder.shape[0]

    def exchange(faces, sent):
        far = lax.ppermute(sent, AXES, reach)
        oth = lax.ppermute(faces, AXES, swap)
        post = lax.ppermute(far, AXES, swap)
        return faces, oth, far, post

    v, f, k, c, kind = (x.reshape(SLOTS * SPAN, LAYER) for x in (v, f, k, c, kind))
    five = jax.ShapeDtypeStruct((5, LAYER, 128), F32)
    twelve = jax.ShapeDtypeStruct((12, SPAN, 128), F32)
    sent_first = jax.ShapeDtypeStruct((5, SPAN, 128), F32)
    sent_later = jax.ShapeDtypeStruct((SPAN, 128), F32)
    landing = pltpu.VMEM((SLOTS * SPAN, LAYER), F32)
    scalars, own, faces = call(
        collect_kernel,
        [pltpu.SMEM((6,), jnp.int32), pltpu.VMEM((3, LAYER, 128), F32), pltpu.VMEM(twelve.shape, F32)],
        [holder.reshape(patches // 128, 128), v, k, kind],
        specs=[HBM] * 4,
        leading=[],
        out_specs=[SMEM, VMEM, VMEM],
        scratch=[pltpu.VMEM((patches // 128, 128), jnp.int32), landing, landing]
        + [pltpu.VMEM((SLOTS * SPAN, LAYER), jnp.int32), pltpu.SemaphoreType.DMA((4,))],
        name="collect",
        limit=COLLECT_LIMIT,
    )
    own_rest = call(
        collect_rest_kernel,
        pltpu.VMEM((2, LAYER, 128), F32),
        [f, c],
        specs=[HBM] * 2,
        leading=[],
        out_specs=VMEM,
        scratch=[landing, landing, pltpu.SemaphoreType.DMA((2,))],
        name="collect_rest",
        limit=COLLECT_LIMIT,
    )
    oth, own_rest = lax.optimization_barrier((lax.ppermute(faces, AXES, swap), own_rest))
    faces, sent = call(
        face_window_kernel,
        [twelve, sent_first],
        [scalars, faces, oth],
        name="face_window",
    )
    sent, own, own_rest = lax.optimization_barrier((sent, own, own_rest))
    far = lax.ppermute(sent, AXES, reach)
    oth = lax.ppermute(faces, AXES, swap)
    window, inner = call(
        window_kernel,
        [five, five],
        [scalars, own, lax.ppermute(own, AXES, swap), own_rest, lax.ppermute(own_rest, AXES, swap)],
        name="window",
    )
    far, window, inner = lax.optimization_barrier((far, window, inner))
    post = lax.ppermute(far, AXES, swap)
    coefficients = jax.ShapeDtypeStruct((6, LAYER, 128), F32)
    wv, wf, wd, wg, edge, faces, *sent = call(
        functools.partial(first_kernel, patches // 4),
        [FIELD, FIELD, FIELD, coefficients, FACES, FACES, sent_later],
        [scalars, window, inner, faces, oth, far, post],
        scratch=[pltpu.VMEM((3, 4, SPAN, 128), F32), PADDED, pltpu.VMEM((2, SPAN, 128), F32)],
        name="first",
    )
    for shade, more in ((1, [sent_later]), (0, [sent_later]), (1, [])):
        wv, faces, *sent = call(
            functools.partial(sweep_kernel, shade),
            [FIELD, FACES] + more,
            [scalars, wv, wf, wg, *exchange(faces, *sent)],
            scratch=[GHOSTS, PADDED],
            name="sweep",
        )
    blocks, cross = call(
        residual_kernel,
        [jax.ShapeDtypeStruct((176, 128), F32), jax.ShapeDtypeStruct((16, 128), F32)],
        [scalars, wv, wf, wg, wd, edge, faces],
        scratch=[GHOSTS, PADDED, pltpu.VMEM((2, SPAN, 128), F32)],
        name="residual",
    )
    beside = [(i, i - 5) for i in range(6, devices, 2)] + [(i, i + 1) for i in range(1, devices - 1, 2)]
    both = jnp.stack([blocks, lax.ppermute(blocks, AXES, swap)], 0)
    downward = [(i, i - 1) for i in range(2, devices, 2)] + [(i, i - 5) for i in range(5, devices, 2)]
    far = lax.ppermute(both, AXES, downward)
    side = lax.ppermute(cross, AXES, beside)
    far, wv = lax.optimization_barrier((far, wv))
    level = call(
        level_kernel,
        jax.ShapeDtypeStruct((SLOTS, SPAN, LAYER), F32),
        [scalars, wv],
        scratch=[pltpu.VMEM((128, LAYER), F32)],
        name="level",
    )
    side, level = lax.optimization_barrier((side, level))
    side, far = lax.optimization_barrier((side, far))
    post = lax.ppermute(far, AXES, swap)
    side_post = lax.ppermute(side, AXES, swap)
    grid = call(
        coarse_kernel,
        jax.ShapeDtypeStruct((1, SPAN, LAYER), F32),
        [scalars, both, far, post, side, side_post],
        scratch=[pltpu.VMEM((5, 128, 128), F32), pltpu.VMEM((9, 48, 128), F32), pltpu.VMEM((LAYER, 128), F32)],
        name="coarse",
    )
    return level, grid


def solution(mesh):
    spec = P(AXES, None, None)
    return jax.shard_map(
        shards,
        mesh=mesh,
        in_specs=(spec, spec, spec, spec, spec, P()),
        out_specs=(spec, spec),
        check_vma=False,
    )
```
